32 devices in a mesh: views: 4 (over y, x), tiles: 8 (over z, core).
Axes of the slice: x: 2, y: 2, z: 4, core: 2. Of those that a mesh axis runs over, the one named last changes fastest.
Arguments:
- params: float32 [59, 4096], P(None, ('views', 'tiles')), as said below
- first_moment: float32 [59, 4096], P(None, ('views', 'tiles')), may hold values from -6 to 6
- second_moment: float32 [59, 4096], P(None, ('views', 'tiles')), may hold values from 0.5 to 20
- cameras: float32 [4, 6], replicated, may hold values from -0.02 to 0.02
- target: float32 [4, 128, 3, 256], P('views', 'tiles'), may hold values from 0 to 1
- lists: int32 [4, 128, 256], P('views', 'tiles'), may hold values from 0 to 4095, as said below
- lengths: int32 [4, 128], P('views', 'tiles'), may hold values from 32 to 256
Outputs:
- new_params: float32 [59, 4096], P(None, ('views', 'tiles'))
- new_first: float32 [59, 4096], P(None, ('views', 'tiles'))
- new_second: float32 [59, 4096], P(None, ('views', 'tiles'))
The draws below stay inside these ranges and needn't reach their ends.
Inputs may be any that keep to these rules, and one draw needn't show every extreme that they name: Each entry names a Gaussian by its column in params. The lists of the 16 tiles that one device holds (live entries or not) have exactly 128 entries in the columns of each device's shard of params. `params`: the quaternion's first entry is at least 0.6, the means lie in front of every camera, and the opacity logits are at most -2.
All inputs are finite; a program needn't handle non-finite values.
Results may differ from the reference program's by a relative error of at most 0.0003.
Values sent between devices are 32-bit elements; how exact they have to be, the bound alone decides.
A program may use at most 128 MiB of HBM per device.

```python
import math
import jax
import jax.numpy as jnp
import numpy as np
from jax import lax

TILE_DEV = 16
LIST = 256
TILE_SIDE = 16
TILE_COLS = 32
PARAMS = 59
ADAM_STEP = 1000
G_DEV = 128
VIEWS = 4
TILES_VIEW = 128
GAUSS = 4096
PIXELS = 256


def draw_params(key, part):
    key = jax.random.fold_in(key, 11)
    key_list = jax.random.split(key, 9)
    width = TILE_COLS * TILE_SIDE
    height = TILES_VIEW // TILE_COLS * TILE_SIDE
    columns = jnp.arange(GAUSS, dtype=jnp.int32)
    home_tile = columns % G_DEV % TILES_VIEW
    screen_u = (home_tile % TILE_COLS * TILE_SIDE).astype(jnp.float32) + jax.random.uniform(key_list[0], (GAUSS,), jnp.float32, 0.0, float(TILE_SIDE))
    screen_v = (home_tile // TILE_COLS * TILE_SIDE).astype(jnp.float32) + jax.random.uniform(key_list[1], (GAUSS,), jnp.float32, 0.0, float(TILE_SIDE))
    depths = jax.random.uniform(key_list[2], (GAUSS,), jnp.float32, 4.0, 8.0)
    mean_x = (screen_u - 0.5 * width) * depths / width
    mean_y = (screen_v - 0.5 * height) * depths / width
    log_scale = jax.random.uniform(key_list[3], (3, GAUSS), jnp.float32, math.log(0.03), math.log(0.09))
    real_part = jax.random.uniform(key_list[4], (1, GAUSS), jnp.float32, 0.6, 1.0)
    imag_parts = jax.random.uniform(key_list[5], (3, GAUSS), jnp.float32, -0.4, 0.4)
    opacity_logit = jax.random.uniform(key_list[6], (1, GAUSS), jnp.float32, -4.5, -2.0)
    base_color = jax.random.uniform(key_list[7], (3, GAUSS), jnp.float32, -1.0, 1.0)
    higher = 0.25 * jax.random.normal(key_list[8], (45, GAUSS), jnp.float32)
    return jnp.concatenate([mean_x[None], mean_y[None], depths[None], log_scale, real_part, imag_parts, opacity_logit, base_color, higher], axis=0)


def draw_lists(key, part):
    key = jax.random.fold_in(key, 12)
    key_list = jax.random.split(key, 3)
    tile_rows = TILES_VIEW // TILE_COLS
    device_count = VIEWS * (TILES_VIEW // TILE_DEV)
    slot_count = TILE_DEV * LIST
    bucket = slot_count // device_count
    base = jnp.broadcast_to((jnp.arange(slot_count, dtype=jnp.int32) // bucket)[None, :], (device_count, slot_count))
    owners = jax.random.permutation(key_list[0], base, axis=1, independent=True).reshape(VIEWS, TILES_VIEW, LIST)
    shape_here = (VIEWS, TILES_VIEW, LIST)
    tile_ids = jnp.arange(TILES_VIEW, dtype=jnp.int32)[None, :, None]
    step_x = jax.random.randint(key_list[1], shape_here, -1, 2)
    step_y = jax.random.randint(key_list[2], shape_here, -1, 2)
    near_x = jnp.clip(tile_ids % TILE_COLS + step_x, 0, TILE_COLS - 1)
    near_y = jnp.clip(tile_ids // TILE_COLS + step_y, 0, tile_rows - 1)
    return (owners * G_DEV + (near_y * TILE_COLS + near_x) % G_DEV).astype(jnp.int32)


def draw_lengths(key, part):
    key = jax.random.fold_in(key, 13)
    tile_rows = TILES_VIEW // TILE_COLS
    tile_ids = jnp.arange(TILES_VIEW, dtype=jnp.int32)[None, :]
    row_of = tile_ids // TILE_COLS
    central = (row_of >= tile_rows // 4) & (row_of < tile_rows - tile_rows // 4)
    ceiling = jnp.where(central, LIST, LIST // 2)
    raw_draw = jax.random.randint(key, (VIEWS, TILES_VIEW), 0, LIST)
    drawn = LIST // 8 + raw_draw % (ceiling - LIST // 8 + 1)
    return jnp.where(central & (tile_ids % TILE_COLS == 0), LIST, drawn).astype(jnp.int32)


def block_levels(own_key, shape, cuts, low, top_value):
    loudness = 1.0
    for position, parts in cuts:
        heights = jax.random.uniform(jax.random.fold_in(jax.random.fold_in(own_key, 6), position), (parts,), jnp.float32, low / len(cuts), top_value / len(cuts))
        loudness = loudness * jnp.repeat(jnp.exp(heights), shape[position] // parts).reshape((-1,) + (1,) * (len(shape) - 1 - position))
    return loudness


def gaussian(rng, dims, spread, reach, pieces=(), held_as=jnp.bfloat16):
    values = spread * jax.random.normal(rng, dims, jnp.float32)
    if pieces:
        values = values * block_levels(rng, dims, pieces, -0.22, 0.18)
    return jnp.clip(values, -reach, reach).astype(held_as)


def setup_inputs(seed: int = 0) -> dict:
    keys = jax.random.split(jax.random.key(seed), 8)
    params = draw_params(jax.random.fold_in(keys[7], 71), 0)
    first_moment = gaussian(keys[1], (PARAMS, GAUSS), 1.0, 6.0, ((1, 32),), jnp.float32)
    second_moment = jnp.clip(jnp.exp(math.log(20.0) - 3.6888795 * jax.random.uniform(keys[2], (PARAMS, GAUSS), jnp.float32) ** block_levels(keys[2], (PARAMS, GAUSS), ((1, 32),), -0.2, 0.2)), 0.5, 20.0)
    cameras = jnp.clip(jax.random.uniform(keys[3], (VIEWS, 6), jnp.float32, -0.02, 0.02), -0.02, 0.02)
    target = jnp.clip(1.0 * jax.random.uniform(keys[4], (VIEWS, TILES_VIEW, 3, PIXELS), jnp.float32) ** block_levels(keys[4], (VIEWS, TILES_VIEW, 3, PIXELS), ((0, 4), (1, 8)), -0.2, 0.2), 0.0, 1.0)
    lists = draw_lists(jax.random.fold_in(keys[7], 71), 0)
    lengths = draw_lengths(jax.random.fold_in(keys[7], 71), 0)
    return dict(params=params, first_moment=first_moment, second_moment=second_moment, cameras=cameras, target=target, lists=lists, lengths=lengths)


sh_zero = 0.28209479177387814
sh_first = 0.4886025119029199
sh_second = (1.0925484305920792, -1.0925484305920792, 0.31539156525252005, -1.0925484305920792, 0.5462742152960396)
sh_third = (-0.5900435899266435, 2.890611442640554, -0.4570457994644658, 0.3731763325901154, -0.4570457994644658, 1.445305721320277, -0.5900435899266435)
beta_one = 0.9
beta_two = 0.999
adam_eps = 1e-15
learning = np.concatenate([np.full(3, 0.00016), np.full(3, 0.005), np.full(4, 0.001), np.full(1, 0.05), np.full(3, 0.0025), np.full(45, 0.000125)]).astype(np.float32)[:, None]

def matmul_three(left, right):
    return [[left[row_at][0] * right[0][col_at] + left[row_at][1] * right[1][col_at] + left[row_at][2] * right[2][col_at] for col_at in range(3)] for row_at in range(3)]

def camera_rotation(camera):
    cos_a, sin_a = (jnp.cos(camera[0]), jnp.sin(camera[0]))
    cos_b, sin_b = (jnp.cos(camera[1]), jnp.sin(camera[1]))
    cos_c, sin_c = (jnp.cos(camera[2]), jnp.sin(camera[2]))
    around_x = [[1.0, 0.0, 0.0], [0.0, cos_a, -sin_a], [0.0, sin_a, cos_a]]
    around_y = [[cos_b, 0.0, sin_b], [0.0, 1.0, 0.0], [-sin_b, 0.0, cos_b]]
    around_z = [[cos_c, -sin_c, 0.0], [sin_c, cos_c, 0.0], [0.0, 0.0, 1.0]]
    return matmul_three(around_z, matmul_three(around_y, around_x))

def sh_basis(along_x, along_y, along_z):
    square_x, square_y, square_z = (along_x * along_x, along_y * along_y, along_z * along_z)
    both_xy, both_yz, both_xz = (along_x * along_y, along_y * along_z, along_x * along_z)
    return [sh_zero + 0.0 * along_x, -sh_first * along_y, sh_first * along_z, -sh_first * along_x, sh_second[0] * both_xy, sh_second[1] * both_yz, sh_second[2] * (2.0 * square_z - square_x - square_y), sh_second[3] * both_xz, sh_second[4] * (square_x - square_y), sh_third[0] * along_y * (3.0 * square_x - square_y), sh_third[1] * both_xy * along_z, sh_third[2] * along_y * (4.0 * square_z - square_x - square_y), sh_third[3] * along_z * (2.0 * square_z - 3.0 * square_x - 3.0 * square_y), sh_third[4] * along_x * (4.0 * square_z - square_x - square_y), sh_third[5] * along_z * (square_x - square_y), sh_third[6] * along_x * (square_x - 3.0 * square_y)]

def project(params, camera, focal_len, center_x, center_y):
    rotation = camera_rotation(camera)
    means = [params[0], params[1], params[2]]
    point = [rotation[axis_at][0] * means[0] + rotation[axis_at][1] * means[1] + rotation[axis_at][2] * means[2] + camera[3 + axis_at] for axis_at in range(3)]
    inverse_z = 1.0 / point[2]
    screen_u = focal_len * point[0] * inverse_z + center_x
    screen_v = focal_len * point[1] * inverse_z + center_y
    scales = jnp.exp(params[3:6])
    unit_quat = params[6:10] * lax.rsqrt(lax.optimization_barrier(jnp.sum(params[6:10] * params[6:10], axis=0)))
    real_part, imag_x, imag_y, imag_z = (unit_quat[0], unit_quat[1], unit_quat[2], unit_quat[3])
    spin = [[1.0 - 2.0 * (imag_y * imag_y + imag_z * imag_z), 2.0 * (imag_x * imag_y - real_part * imag_z), 2.0 * (imag_x * imag_z + real_part * imag_y)], [2.0 * (imag_x * imag_y + real_part * imag_z), 1.0 - 2.0 * (imag_x * imag_x + imag_z * imag_z), 2.0 * (imag_y * imag_z - real_part * imag_x)], [2.0 * (imag_x * imag_z - real_part * imag_y), 2.0 * (imag_y * imag_z + real_part * imag_x), 1.0 - 2.0 * (imag_x * imag_x + imag_y * imag_y)]]
    turned = matmul_three(rotation, spin)
    shaped = [[turned[row_at][col_at] * scales[col_at] for col_at in range(3)] for row_at in range(3)]
    near_x = [focal_len * inverse_z * shaped[0][col_at] - focal_len * point[0] * inverse_z * inverse_z * shaped[2][col_at] for col_at in range(3)]
    near_y = [focal_len * inverse_z * shaped[1][col_at] - focal_len * point[1] * inverse_z * inverse_z * shaped[2][col_at] for col_at in range(3)]
    cov_a = near_x[0] * near_x[0] + near_x[1] * near_x[1] + near_x[2] * near_x[2] + 0.3
    cov_b = near_x[0] * near_y[0] + near_x[1] * near_y[1] + near_x[2] * near_y[2]
    cov_c = near_y[0] * near_y[0] + near_y[1] * near_y[1] + near_y[2] * near_y[2] + 0.3
    determinant = cov_a * cov_c - cov_b * cov_b
    offset = [means[axis_at] + rotation[0][axis_at] * camera[3] + rotation[1][axis_at] * camera[4] + rotation[2][axis_at] * camera[5] for axis_at in range(3)]
    inverse_len = lax.rsqrt(offset[0] * offset[0] + offset[1] * offset[1] + offset[2] * offset[2])
    basis = sh_basis(offset[0] * inverse_len, offset[1] * inverse_len, offset[2] * inverse_len)
    colors = [0.5 + sum((basis[coef_at] * params[11 + 3 * coef_at + channel] for coef_at in range(16))) for channel in range(3)]
    opacity = jax.nn.sigmoid(params[10])
    return jnp.stack([screen_u, screen_v, cov_c / determinant, -cov_b / determinant, cov_a / determinant, opacity, colors[0], colors[1], colors[2]])

def composite(picked, lengths, target, first_tile):
    tile_count = picked.shape[1]
    list_size = picked.shape[2]
    tile_ids = first_tile + jnp.arange(tile_count, dtype=jnp.int32)
    pixel_ids = jnp.arange(TILE_SIDE * TILE_SIDE, dtype=jnp.int32)
    pixel_x = (tile_ids % TILE_COLS * TILE_SIDE)[:, None] + (pixel_ids % TILE_SIDE)[None, :]
    pixel_y = (tile_ids // TILE_COLS * TILE_SIDE)[:, None] + (pixel_ids // TILE_SIDE)[None, :]
    delta_x = pixel_x.astype(jnp.float32)[:, None, :] + 0.5 - picked[0][:, :, None]
    delta_y = pixel_y.astype(jnp.float32)[:, None, :] + 0.5 - picked[1][:, :, None]
    quadric = picked[2][:, :, None] * delta_x * delta_x + 2.0 * picked[3][:, :, None] * delta_x * delta_y + picked[4][:, :, None] * delta_y * delta_y
    live_mask = jnp.arange(list_size, dtype=jnp.int32)[None, :] < lengths[:, None]
    alphas = jnp.where(live_mask[:, :, None], picked[5][:, :, None] * jnp.exp(-0.5 * quadric), 0.0)
    log_keep = jnp.log1p(-alphas)
    weight = jnp.exp(jnp.cumsum(log_keep, axis=1) - log_keep) * alphas
    render = jnp.stack([lax.optimization_barrier(jnp.sum(weight * picked[6 + channel][:, :, None], axis=1)) for channel in range(3)], axis=1)
    return jnp.sum(jnp.abs(render - target))

def adam_update(params, first_moment, second_moment, gradient):
    new_first = beta_one * first_moment + (1.0 - beta_one) * gradient
    new_second = beta_two * second_moment + (1.0 - beta_two) * gradient * gradient
    step_size = learning * (new_first / (1.0 - beta_one ** ADAM_STEP))
    new_params = params - step_size / (jnp.sqrt(new_second / (1.0 - beta_two ** ADAM_STEP)) + adam_eps)
    return (new_params, new_first, new_second)

def view_gradient(projected, lists, lengths, target):
    tile_rows = lists.shape[0] // TILE_COLS
    blocks = (lists.reshape(tile_rows, TILE_COLS, -1), lengths.reshape(tile_rows, TILE_COLS), target.reshape(tile_rows, TILE_COLS, 3, -1), jnp.arange(tile_rows, dtype=jnp.int32) * TILE_COLS)

    def one_block(dense_rows, block):
        indices, block_len, block_target, first_tile = block
        picked = jnp.take(projected, indices, axis=1)
        _, pull_block = jax.vjp(lambda chosen: composite(chosen, block_len, block_target, first_tile), picked)
        picked_grad = pull_block(jnp.ones((), projected.dtype))[0]
        dense_rows = dense_rows.at[:, indices.reshape(-1)].add(picked_grad.reshape(projected.shape[0], -1))
        return (dense_rows, None)
    dense_rows, _ = lax.scan(one_block, jnp.zeros_like(projected), blocks)
    return dense_rows

def reference(params, first_moment, second_moment, cameras, target, lists, lengths):
    width = TILE_COLS * TILE_SIDE
    height = TILES_VIEW // TILE_COLS * TILE_SIDE
    focal_len = float(width)

    def all_views(values):
        return jnp.stack([project(values, cameras[camera_at], focal_len, 0.5 * width, 0.5 * height) for camera_at in range(VIEWS)])
    projected, pullback = jax.vjp(all_views, params)
    row_grads = jnp.stack([view_gradient(projected[camera_at], lists[camera_at], lengths[camera_at], target[camera_at]) for camera_at in range(VIEWS)])
    gradient = pullback(row_grads)[0]
    return adam_update(params, first_moment, second_moment, gradient)
```

```python
import jax
import jax.numpy as jnp
import numpy as np
from jax import lax
from jax.experimental import pallas as pl
from jax.experimental.pallas import tpu as pltpu
from jax.sharding import PartitionSpec as P

TILE_SIDE = 16
TILE_COLS = 32
ADAM_STEP = 1000


sh_zero = 0.28209479177387814
sh_first = 0.4886025119029199
sh_second = (
    1.0925484305920792,
    -1.0925484305920792,
    0.31539156525252005,
    -1.0925484305920792,
    0.5462742152960396,
)
sh_third = (
    -0.5900435899266435,
    2.890611442640554,
    -0.4570457994644658,
    0.3731763325901154,
    -0.4570457994644658,
    1.445305721320277,
    -0.5900435899266435,
)
beta_one = 0.9
beta_two = 0.999
adam_eps = 1e-15
learning = np.concatenate(
    [
        np.full(3, 0.00016),
        np.full(3, 0.005),
        np.full(4, 0.001),
        np.full(1, 0.05),
        np.full(3, 0.0025),
        np.full(45, 0.000125),
    ]
).astype(np.float32)[:, None]


def matmul_three(left, right):
    return [
        [
            left[row_at][0] * right[0][col_at]
            + left[row_at][1] * right[1][col_at]
            + left[row_at][2] * right[2][col_at]
            for col_at in range(3)
        ]
        for row_at in range(3)
    ]


def camera_rotation(camera):
    cos_a, sin_a = (jnp.cos(camera[0]), jnp.sin(camera[0]))
    cos_b, sin_b = (jnp.cos(camera[1]), jnp.sin(camera[1]))
    cos_c, sin_c = (jnp.cos(camera[2]), jnp.sin(camera[2]))
    around_x = [[1.0, 0.0, 0.0], [0.0, cos_a, -sin_a], [0.0, sin_a, cos_a]]
    around_y = [[cos_b, 0.0, sin_b], [0.0, 1.0, 0.0], [-sin_b, 0.0, cos_b]]
    around_z = [[cos_c, -sin_c, 0.0], [sin_c, cos_c, 0.0], [0.0, 0.0, 1.0]]
    return matmul_three(around_z, matmul_three(around_y, around_x))


def sh_basis(along_x, along_y, along_z):
    square_x, square_y, square_z = (along_x * along_x, along_y * along_y, along_z * along_z)
    both_xy, both_yz, both_xz = (along_x * along_y, along_y * along_z, along_x * along_z)
    return [
        sh_zero + 0.0 * along_x,
        -sh_first * along_y,
        sh_first * along_z,
        -sh_first * along_x,
        sh_second[0] * both_xy,
        sh_second[1] * both_yz,
        sh_second[2] * (2.0 * square_z - square_x - square_y),
        sh_second[3] * both_xz,
        sh_second[4] * (square_x - square_y),
        sh_third[0] * along_y * (3.0 * square_x - square_y),
        sh_third[1] * both_xy * along_z,
        sh_third[2] * along_y * (4.0 * square_z - square_x - square_y),
        sh_third[3] * along_z * (2.0 * square_z - 3.0 * square_x - 3.0 * square_y),
        sh_third[4] * along_x * (4.0 * square_z - square_x - square_y),
        sh_third[5] * along_z * (square_x - square_y),
        sh_third[6] * along_x * (square_x - 3.0 * square_y),
    ]


def project(rows, camera, focal_len, center_x, center_y):
    rotation = camera_rotation(camera)
    means = rows[0:3]
    point = [
        rotation[axis_at][0] * means[0]
        + rotation[axis_at][1] * means[1]
        + rotation[axis_at][2] * means[2]
        + camera[3 + axis_at]
        for axis_at in range(3)
    ]
    inverse_z = 1.0 / point[2]
    screen_u = focal_len * point[0] * inverse_z + center_x
    screen_v = focal_len * point[1] * inverse_z + center_y
    scales = [jnp.exp(value) for value in rows[3:6]]
    norm = rows[6] * rows[6] + rows[7] * rows[7] + rows[8] * rows[8] + rows[9] * rows[9]
    inverse_norm = lax.rsqrt(norm)
    real_part, imag_x, imag_y, imag_z = [value * inverse_norm for value in rows[6:10]]
    spin = [
        [
            1.0 - 2.0 * (imag_y * imag_y + imag_z * imag_z),
            2.0 * (imag_x * imag_y - real_part * imag_z),
            2.0 * (imag_x * imag_z + real_part * imag_y),
        ],
        [
            2.0 * (imag_x * imag_y + real_part * imag_z),
            1.0 - 2.0 * (imag_x * imag_x + imag_z * imag_z),
            2.0 * (imag_y * imag_z - real_part * imag_x),
        ],
        [
            2.0 * (imag_x * imag_z - real_part * imag_y),
            2.0 * (imag_y * imag_z + real_part * imag_x),
            1.0 - 2.0 * (imag_x * imag_x + imag_y * imag_y),
        ],
    ]
    turned = matmul_three(rotation, spin)
    shaped = [
        [turned[row_at][col_at] * scales[col_at] for col_at in range(3)] for row_at in range(3)
    ]
    near_x = [
        focal_len * inverse_z * shaped[0][col_at]
        - focal_len * point[0] * inverse_z * inverse_z * shaped[2][col_at]
        for col_at in range(3)
    ]
    near_y = [
        focal_len * inverse_z * shaped[1][col_at]
        - focal_len * point[1] * inverse_z * inverse_z * shaped[2][col_at]
        for col_at in range(3)
    ]
    cov_a = near_x[0] * near_x[0] + near_x[1] * near_x[1] + near_x[2] * near_x[2] + 0.3
    cov_b = near_x[0] * near_y[0] + near_x[1] * near_y[1] + near_x[2] * near_y[2]
    cov_c = near_y[0] * near_y[0] + near_y[1] * near_y[1] + near_y[2] * near_y[2] + 0.3
    determinant = cov_a * cov_c - cov_b * cov_b
    offset = [
        means[axis_at]
        + rotation[0][axis_at] * camera[3]
        + rotation[1][axis_at] * camera[4]
        + rotation[2][axis_at] * camera[5]
        for axis_at in range(3)
    ]
    inverse_len = lax.rsqrt(offset[0] * offset[0] + offset[1] * offset[1] + offset[2] * offset[2])
    basis = sh_basis(offset[0] * inverse_len, offset[1] * inverse_len, offset[2] * inverse_len)
    colors = [
        0.5 + sum((basis[coef_at] * rows[11 + 3 * coef_at + channel] for coef_at in range(16)))
        for channel in range(3)
    ]
    return (
        screen_u,
        screen_v,
        cov_c / determinant,
        -cov_b / determinant,
        cov_a / determinant,
        colors[0],
        colors[1],
        colors[2],
    )


def exchange(source_of, landing_ref, send_sem, recv_sem, peers, tile_groups, me):
    def copy_to(step):
        peer = lax.rem(me + step, peers)
        return pltpu.make_async_remote_copy(
            src_ref=source_of(peer),
            dst_ref=landing_ref.at[me],
            send_sem=send_sem.at[step],
            recv_sem=recv_sem.at[step],
            device_id=(peer // tile_groups, lax.rem(peer, tile_groups)),
            device_id_type=pl.DeviceIdType.MESH,
        )

    def start(step, carry):
        copy_to(step).start()
        return carry

    def finish(step, carry):
        copy_to(step).wait()
        return carry

    return (
        lambda: lax.fori_loop(1, peers, start, 0),
        lambda: lax.fori_loop(1, peers, finish, 0),
    )


def greet(peers, tile_groups, me):
    barrier = pltpu.get_barrier_semaphore()

    def one(step, carry):
        peer = lax.rem(me + step, peers)
        pl.semaphore_signal(
            barrier,
            inc=1,
            device_id=(peer // tile_groups, lax.rem(peer, tile_groups)),
            device_id_type=pl.DeviceIdType.MESH,
        )
        return carry

    lax.fori_loop(1, peers, one, 0)
    return lambda: pl.semaphore_wait(barrier, peers - 1)


def camera_columns(cameras_ref):
    return [cameras_ref[:, at : at + 1] for at in range(6)]


def sigmoid(value):
    return 1.0 / (1.0 + jnp.exp(-value))


def project_kernel(
    peers, tile_groups, width, height, cameras_ref, params_ref, table_ref, rows_ref, send_sem, recv_sem
):
    my_view = lax.axis_index("views")
    me = my_view * tile_groups + lax.axis_index("tiles")
    everyone_here = greet(peers, tile_groups, me)
    view_count = rows_ref.shape[0]
    owned = params_ref.shape[1]
    values = [params_ref[at : at + 1, :] for at in range(59)]
    made = project(
        values, camera_columns(cameras_ref), float(width), 0.5 * width, 0.5 * height
    )
    opacity = jnp.broadcast_to(sigmoid(values[10]), (view_count, owned))
    for row_at, value in enumerate(made[:5] + (opacity,) + made[5:]):
        rows_ref[:, row_at, :] = value
    everyone_here()
    start, finish = exchange(
        lambda peer: rows_ref.at[peer // tile_groups],
        table_ref,
        send_sem,
        recv_sem,
        peers,
        tile_groups,
        me,
    )
    start()
    table_ref[pl.ds(me, 1)] = rows_ref[pl.ds(my_view, 1)]
    finish()


def collect_kernel(peers, tile_groups, dense_ref, out_ref, landing_ref, send_sem, recv_sem):
    me = lax.axis_index("views") * tile_groups + lax.axis_index("tiles")
    everyone_here = greet(peers, tile_groups, me)
    everyone_here()
    start, finish = exchange(
        lambda peer: dense_ref.at[peer], landing_ref, send_sem, recv_sem, peers, tile_groups, me
    )
    start()
    landing_ref[pl.ds(me, 1)] = dense_ref[pl.ds(me, 1)]
    finish()
    for view_at in range(out_ref.shape[0]):
        out_ref[view_at] = jnp.sum(
            landing_ref[view_at * tile_groups : (view_at + 1) * tile_groups], axis=0
        )


def fold(value):
    return value[0:8] + value[8:16]


def composite_kernel(
    first_tile_ref,
    lengths_ref,
    lists_ref,
    target_ref,
    table_ref,
    dense_ref,
    picked,
    keeps,
    suffix,
    before,
    after,
    alpha_s,
    ratio_s,
    flow_s,
    chosen,
    spread,
):
    f32, bf16 = jnp.float32, jnp.bfloat16
    tile_dev, list_size = lists_ref.shape
    peers, _, owned = table_ref.shape
    per_owner = owned // 128
    halves = list_size // 128
    entries = lists_ref[...]
    block_of = entries >> 7
    column_of = entries & 127

    def gather_from(owner, carry):
        carry = list(carry)
        for part in range(per_owner):
            lanes = slice(part * 128, part * 128 + 128)
            for half in range(halves):
                here = slice(half * 128, half * 128 + 128)
                mask = block_of[:, here] == owner * per_owner + part
                column = column_of[:, here]
                for row_at in range(9):
                    line = table_ref[owner, row_at : row_at + 1, lanes]
                    got = jnp.take_along_axis(
                        jnp.broadcast_to(line, (tile_dev, 128)),
                        column,
                        axis=1,
                        mode="promise_in_bounds",
                    )
                    slot = half * 9 + row_at
                    carry[slot] = jnp.where(mask, got, carry[slot])
        return tuple(carry)

    zeros = tuple(jnp.zeros((tile_dev, 128), f32) for _ in range(halves * 9))
    gathered = lax.fori_loop(0, peers, gather_from, zeros)
    for half in range(halves):
        for row_at in range(9):
            picked[row_at, :, half * 128 : half * 128 + 128] = gathered[half * 9 + row_at]

    row_ids = lax.broadcasted_iota(jnp.int32, (list_size, list_size), 0)
    col_ids = lax.broadcasted_iota(jnp.int32, (list_size, list_size), 1)
    for piece in range(3):
        before[piece * list_size : (piece + 1) * list_size, :] = (row_ids < col_ids).astype(f32).astype(bf16)
    for piece in range(2):
        after[piece * list_size : (piece + 1) * list_size, :] = (row_ids > col_ids).astype(f32).astype(bf16)
    spread[...] = jnp.zeros_like(spread)
    lane_ids = lax.broadcasted_iota(jnp.int32, (1, list_size), 1)
    pixel_ids = lax.broadcasted_iota(jnp.int32, (16, list_size), 0).astype(f32)
    column_ids = lax.broadcasted_iota(jnp.int32, (128, list_size), 0)
    first_tile = first_tile_ref[0]
    group = spread.shape[1] // 32

    def one_tile(tile_at, carry):
        tile_id = first_tile + tile_at
        left = (tile_id % TILE_COLS * TILE_SIDE).astype(f32) + 0.5
        top = (tile_id // TILE_COLS * TILE_SIDE).astype(f32) + 0.5
        u, v, con_a, con_b, con_c, opacity, red, green, blue = [
            picked[row_at, pl.ds(tile_at, 1), :] for row_at in range(9)
        ]
        opacity = jnp.where(lane_ids < lengths_ref[tile_at], opacity, 0.0)
        delta_x = (pixel_ids + left) - u
        part_a = (-0.5 * con_a) * delta_x * delta_x
        part_b = -con_b * delta_x
        half_c = -0.5 * con_c
        deltas_y = [(top + float(line)) - v for line in range(TILE_SIDE)]
        for line in range(TILE_SIDE):
            here = slice(line * 16, line * 16 + 16)
            delta_y = deltas_y[line]
            alphas = opacity * jnp.exp(part_a + delta_y * (part_b + half_c * delta_y))
            log_keep = jnp.log(1.0 - alphas)
            high = log_keep.astype(bf16)
            rest = log_keep - high.astype(f32)
            middle = rest.astype(bf16)
            low = (rest - middle.astype(f32)).astype(bf16)
            keeps[here, 0:list_size] = high
            keeps[here, list_size : 2 * list_size] = middle
            keeps[here, 2 * list_size : 3 * list_size] = low
            alpha_s[here, :] = alphas
            ratio_s[here, :] = alphas * jnp.exp(-log_keep)
        passed = jnp.dot(keeps[...], before[...], preferred_element_type=f32)
        wanted = jnp.concatenate(
            [target_ref[tile_at], jnp.zeros((5, TILE_SIDE * TILE_SIDE), f32)], axis=0
        ).T
        color_sums = [jnp.zeros((8, list_size), f32) for _ in range(3)]
        for line in range(TILE_SIDE):
            here = slice(line * 16, line * 16 + 16)
            weight = jnp.exp(passed[here]) * alpha_s[here, :]
            signs = []
            for channel, color in enumerate((red, green, blue)):
                gap = jnp.sum(weight * color, axis=1, keepdims=True) - wanted[here, channel : channel + 1]
                sign = jnp.where(gap > 0.0, 1.0, jnp.where(gap < 0.0, -1.0, 0.0))
                signs.append(sign)
                color_sums[channel] = color_sums[channel] + fold(weight * sign)
            flow = weight * (signs[0] * red + signs[1] * green + signs[2] * blue)
            high = flow.astype(bf16)
            suffix[here, 0:list_size] = high
            suffix[here, list_size : 2 * list_size] = (flow - high.astype(f32)).astype(bf16)
            flow_s[here, :] = flow
        behind = jnp.dot(suffix[...], after[...], preferred_element_type=f32)
        sums = [jnp.zeros((8, list_size), f32) for _ in range(6)]
        for line in range(TILE_SIDE):
            here = slice(line * 16, line * 16 + 16)
            delta_y = deltas_y[line]
            pull = flow_s[here, :] - behind[here] * ratio_s[here, :]
            pull_x = pull * delta_x
            pull_xx = fold(pull_x * delta_x)
            pull_x = fold(pull_x)
            pull = fold(pull)
            pull_y = pull * delta_y
            terms = (pull, pull_x, pull_y, pull_xx, pull_x * delta_y, pull_y * delta_y)
            sums = [total + term for total, term in zip(sums, terms)]
        flat, by_x, by_y, by_xx, by_xy, by_yy = [
            jnp.sum(total, axis=0, keepdims=True) for total in sums
        ]
        grads = jnp.concatenate(
            [
                con_a * by_x + con_b * by_y,
                con_b * by_x + con_c * by_y,
                -0.5 * by_xx,
                -by_xy,
                -0.5 * by_yy,
                flat,
            ]
            + [jnp.sum(total, axis=0, keepdims=True) for total in color_sums]
            + [jnp.zeros((7, list_size), f32)],
            axis=0,
        )
        high = grads.astype(bf16).astype(f32)
        pieces = jnp.concatenate([high, grads - high], axis=0)
        ids = lists_ref[pl.ds(tile_at, 1), :]
        owner = ids >> 7
        one_hot = (column_ids == (ids & 127)).astype(f32).astype(bf16)

        def spread_group(group_at, carry):
            for at in range(group):
                mask = owner == group_at * group + at
                chosen[at * 32 : at * 32 + 32, :] = jnp.where(mask, pieces, 0.0).astype(bf16)
            spread[group_at] += lax.dot_general(
                chosen[...], one_hot, (((1,), (1,)), ((), ())), preferred_element_type=f32
            )
            return carry

        if spread.shape[0] == 1:
            spread_group(0, 0)
        else:
            lax.fori_loop(0, spread.shape[0], spread_group, 0)
        return carry

    lax.fori_loop(0, tile_dev, one_tile, 0)

    owners_here = group // per_owner

    def finish_group(group_at, carry):
        for at in range(group):
            both = spread[group_at, at * 32 : at * 32 + 32, :]
            lanes = at % per_owner * 128
            dense_ref[group_at * owners_here + at // per_owner, :, lanes : lanes + 128] = (
                both[0:9] + both[16:25]
            )
        return carry

    lax.fori_loop(0, spread.shape[0], finish_group, 0)


def update_kernel(
    width,
    height,
    cameras_ref,
    rates_ref,
    grads_ref,
    params_ref,
    first_ref,
    second_ref,
    new_params_ref,
    new_first_ref,
    new_second_ref,
):
    camera = camera_columns(cameras_ref)
    values = [params_ref[at : at + 1, :] for at in range(59)]
    _, pullback = jax.vjp(
        lambda rows: project(rows, camera, float(width), 0.5 * width, 0.5 * height), values
    )
    given = [grads_ref[:, row_at, :] for row_at in range(9)]
    grads = list(pullback(tuple(given[:5] + given[6:]))[0])
    grads[10] = jnp.sum(given[5], axis=0, keepdims=True) * (1.0 - sigmoid(values[10]))
    for at in range(59):
        new_first_ref[at : at + 1, :] = grads[at]
    gradient = new_first_ref[...]
    new_first = beta_one * first_ref[...] + (1.0 - beta_one) * gradient
    new_second = beta_two * second_ref[...] + (1.0 - beta_two) * gradient * gradient
    new_first_ref[...] = new_first
    new_second_ref[...] = new_second
    step_size = rates_ref[...] * (new_first / (1.0 - beta_one**ADAM_STEP))
    new_params_ref[...] = params_ref[...] - step_size / (
        jnp.sqrt(new_second / (1.0 - beta_two**ADAM_STEP)) + adam_eps
    )


def in_vmem(count):
    return [pl.BlockSpec(memory_space=pltpu.VMEM)] * count


def per_device(params, first_moment, second_moment, cameras, target, lists, lengths):
    f32, bf16 = jnp.float32, jnp.bfloat16
    view_count = lax.axis_size("views")
    tile_groups = lax.axis_size("tiles")
    peers = view_count * tile_groups
    owned = params.shape[1]
    tile_dev = target.shape[1]
    list_size = lists.shape[2]
    pixels = target.shape[3]
    width = TILE_COLS * TILE_SIDE
    height = tile_dev * tile_groups // TILE_COLS * TILE_SIDE
    limit = 56 * 1024 * 1024

    table = pl.pallas_call(
        lambda *refs: project_kernel(peers, tile_groups, width, height, *refs),
        out_shape=jax.ShapeDtypeStruct((peers, 9, owned), f32),
        in_specs=in_vmem(2),
        out_specs=pl.BlockSpec(memory_space=pltpu.VMEM),
        scratch_shapes=[
            pltpu.VMEM((view_count, 9, owned), f32),
            pltpu.SemaphoreType.DMA((peers,)),
            pltpu.SemaphoreType.DMA((peers,)),
        ],
        compiler_params=pltpu.CompilerParams(
            collective_id=0, has_side_effects=True, vmem_limit_bytes=limit
        ),
        name="project_rows",
    )(cameras, params)

    blocks = peers * owned // 128
    group = 32
    first_tile = (lax.axis_index("tiles") * tile_dev).astype(jnp.int32).reshape(1)
    dense = pl.pallas_call(
        composite_kernel,
        out_shape=jax.ShapeDtypeStruct((peers, 9, owned), f32),
        in_specs=[pl.BlockSpec(memory_space=pltpu.SMEM)] * 2 + in_vmem(3),
        out_specs=pl.BlockSpec(memory_space=pltpu.VMEM),
        scratch_shapes=[
            pltpu.VMEM((9, tile_dev, list_size), f32),
            pltpu.VMEM((pixels, 3 * list_size), bf16),
            pltpu.VMEM((pixels, 2 * list_size), bf16),
            pltpu.VMEM((3 * list_size, list_size), bf16),
            pltpu.VMEM((2 * list_size, list_size), bf16),
            pltpu.VMEM((pixels, list_size), f32),
            pltpu.VMEM((pixels, list_size), f32),
            pltpu.VMEM((pixels, list_size), f32),
            pltpu.VMEM((group * 32, list_size), bf16),
            pltpu.VMEM((blocks // group, group * 32, 128), f32),
        ],
        compiler_params=pltpu.CompilerParams(vmem_limit_bytes=limit),
        name="composite_tiles",
    )(first_tile, lengths[0], lists[0], target[0], table)

    row_grads = pl.pallas_call(
        lambda *refs: collect_kernel(peers, tile_groups, *refs),
        out_shape=jax.ShapeDtypeStruct((view_count, 9, owned), f32),
        in_specs=in_vmem(1),
        out_specs=pl.BlockSpec(memory_space=pltpu.VMEM),
        scratch_shapes=[
            pltpu.VMEM((peers, 9, owned), f32),
            pltpu.SemaphoreType.DMA((peers,)),
            pltpu.SemaphoreType.DMA((peers,)),
        ],
        compiler_params=pltpu.CompilerParams(
            collective_id=1, has_side_effects=True, vmem_limit_bytes=limit
        ),
        name="collect_grads",
    )(dense)

    like = jax.ShapeDtypeStruct(params.shape, f32)
    return pl.pallas_call(
        lambda *refs: update_kernel(width, height, *refs),
        out_shape=(like, like, like),
        in_specs=in_vmem(6),
        out_specs=tuple(in_vmem(3)),
        compiler_params=pltpu.CompilerParams(vmem_limit_bytes=limit),
        name="update_gaussians",
    )(cameras, jnp.asarray(learning), row_grads, params, first_moment, second_moment)


def solution(mesh):
    placed = (
        P(None, ("views", "tiles")),
        P(None, ("views", "tiles")),
        P(None, ("views", "tiles")),
        P(),
        P("views", "tiles", None, None),
        P("views", "tiles", None),
        P("views", "tiles"),
    )
    return jax.shard_map(
        per_device,
        mesh=mesh,
        in_specs=placed,
        out_specs=(
            P(None, ("views", "tiles")),
            P(None, ("views", "tiles")),
            P(None, ("views", "tiles")),
        ),
        check_vma=False,
    )
```

```python
import jax
import jax.numpy as jnp
import numpy as np
from jax import lax
from jax.experimental import pallas as pl
from jax.experimental.pallas import tpu as pltpu
from jax.sharding import PartitionSpec as P

TILE_SIDE = 16
TILE_COLS = 32
ADAM_STEP = 1000


sh_zero = 0.28209479177387814
sh_first = 0.4886025119029199
sh_second = (
    1.0925484305920792,
    -1.0925484305920792,
    0.31539156525252005,
    -1.0925484305920792,
    0.5462742152960396,
)
sh_third = (
    -0.5900435899266435,
    2.890611442640554,
    -0.4570457994644658,
    0.3731763325901154,
    -0.4570457994644658,
    1.445305721320277,
    -0.5900435899266435,
)
beta_one = 0.9
beta_two = 0.999
adam_eps = 1e-15
learning = np.concatenate(
    [
        np.full(3, 0.00016),
        np.full(3, 0.005),
        np.full(4, 0.001),
        np.full(1, 0.05),
        np.full(3, 0.0025),
        np.full(45, 0.000125),
    ]
).astype(np.float32)[:, None]


def matmul_three(left, right):
    return [
        [
            left[row_at][0] * right[0][col_at]
            + left[row_at][1] * right[1][col_at]
            + left[row_at][2] * right[2][col_at]
            for col_at in range(3)
        ]
        for row_at in range(3)
    ]


def camera_rotation(camera):
    cos_a, sin_a = (jnp.cos(camera[0]), jnp.sin(camera[0]))
    cos_b, sin_b = (jnp.cos(camera[1]), jnp.sin(camera[1]))
    cos_c, sin_c = (jnp.cos(camera[2]), jnp.sin(camera[2]))
    around_x = [[1.0, 0.0, 0.0], [0.0, cos_a, -sin_a], [0.0, sin_a, cos_a]]
    around_y = [[cos_b, 0.0, sin_b], [0.0, 1.0, 0.0], [-sin_b, 0.0, cos_b]]
    around_z = [[cos_c, -sin_c, 0.0], [sin_c, cos_c, 0.0], [0.0, 0.0, 1.0]]
    return matmul_three(around_z, matmul_three(around_y, around_x))


def sh_basis(along_x, along_y, along_z):
    square_x, square_y, square_z = (along_x * along_x, along_y * along_y, along_z * along_z)
    both_xy, both_yz, both_xz = (along_x * along_y, along_y * along_z, along_x * along_z)
    return [
        sh_zero + 0.0 * along_x,
        -sh_first * along_y,
        sh_first * along_z,
        -sh_first * along_x,
        sh_second[0] * both_xy,
        sh_second[1] * both_yz,
        sh_second[2] * (2.0 * square_z - square_x - square_y),
        sh_second[3] * both_xz,
        sh_second[4] * (square_x - square_y),
        sh_third[0] * along_y * (3.0 * square_x - square_y),
        sh_third[1] * both_xy * along_z,
        sh_third[2] * along_y * (4.0 * square_z - square_x - square_y),
        sh_third[3] * along_z * (2.0 * square_z - 3.0 * square_x - 3.0 * square_y),
        sh_third[4] * along_x * (4.0 * square_z - square_x - square_y),
        sh_third[5] * along_z * (square_x - square_y),
        sh_third[6] * along_x * (square_x - 3.0 * square_y),
    ]


def project(rows, camera, focal_len, center_x, center_y):
    rotation = camera_rotation(camera)
    means = rows[0:3]
    point = [
        rotation[axis_at][0] * means[0]
        + rotation[axis_at][1] * means[1]
        + rotation[axis_at][2] * means[2]
        + camera[3 + axis_at]
        for axis_at in range(3)
    ]
    inverse_z = 1.0 / point[2]
    screen_u = focal_len * point[0] * inverse_z + center_x
    screen_v = focal_len * point[1] * inverse_z + center_y
    scales = [jnp.exp(value) for value in rows[3:6]]
    norm = rows[6] * rows[6] + rows[7] * rows[7] + rows[8] * rows[8] + rows[9] * rows[9]
    inverse_norm = lax.rsqrt(norm)
    real_part, imag_x, imag_y, imag_z = [value * inverse_norm for value in rows[6:10]]
    spin = [
        [
            1.0 - 2.0 * (imag_y * imag_y + imag_z * imag_z),
            2.0 * (imag_x * imag_y - real_part * imag_z),
            2.0 * (imag_x * imag_z + real_part * imag_y),
        ],
        [
            2.0 * (imag_x * imag_y + real_part * imag_z),
            1.0 - 2.0 * (imag_x * imag_x + imag_z * imag_z),
            2.0 * (imag_y * imag_z - real_part * imag_x),
        ],
        [
            2.0 * (imag_x * imag_z - real_part * imag_y),
            2.0 * (imag_y * imag_z + real_part * imag_x),
            1.0 - 2.0 * (imag_x * imag_x + imag_y * imag_y),
        ],
    ]
    turned = matmul_three(rotation, spin)
    shaped = [
        [turned[row_at][col_at] * scales[col_at] for col_at in range(3)] for row_at in range(3)
    ]
    near_x = [
        focal_len * inverse_z * shaped[0][col_at]
        - focal_len * point[0] * inverse_z * inverse_z * shaped[2][col_at]
        for col_at in range(3)
    ]
    near_y = [
        focal_len * inverse_z * shaped[1][col_at]
        - focal_len * point[1] * inverse_z * inverse_z * shaped[2][col_at]
        for col_at in range(3)
    ]
    cov_a = near_x[0] * near_x[0] + near_x[1] * near_x[1] + near_x[2] * near_x[2] + 0.3
    cov_b = near_x[0] * near_y[0] + near_x[1] * near_y[1] + near_x[2] * near_y[2]
    cov_c = near_y[0] * near_y[0] + near_y[1] * near_y[1] + near_y[2] * near_y[2] + 0.3
    determinant = cov_a * cov_c - cov_b * cov_b
    offset = [
        means[axis_at]
        + rotation[0][axis_at] * camera[3]
        + rotation[1][axis_at] * camera[4]
        + rotation[2][axis_at] * camera[5]
        for axis_at in range(3)
    ]
    inverse_len = lax.rsqrt(offset[0] * offset[0] + offset[1] * offset[1] + offset[2] * offset[2])
    basis = sh_basis(offset[0] * inverse_len, offset[1] * inverse_len, offset[2] * inverse_len)
    colors = [
        0.5 + sum((basis[coef_at] * rows[11 + 3 * coef_at + channel] for coef_at in range(16)))
        for channel in range(3)
    ]
    return (
        screen_u,
        screen_v,
        cov_c / determinant,
        -cov_b / determinant,
        cov_a / determinant,
        colors[0],
        colors[1],
        colors[2],
    )


def rotated(start, count):
    return [lax.rem(start + step, count) for step in range(count)]


def greet(views, tiles):
    barrier = pltpu.get_barrier_semaphore()
    here = (views[0], tiles[0])
    others = [(view, here[1]) for view in views[1:]] + [(here[0], tile) for tile in tiles[1:]]
    for device in others:
        pl.semaphore_signal(
            barrier, inc=1, device_id=device, device_id_type=pl.DeviceIdType.MESH
        )
    return lambda: pl.semaphore_wait(barrier, len(others))


def send(source, landing, send_sem, recv_sem, device):
    copy = pltpu.make_async_remote_copy(
        src_ref=source,
        dst_ref=landing,
        send_sem=send_sem,
        recv_sem=recv_sem,
        device_id=device,
        device_id_type=pl.DeviceIdType.MESH,
    )
    copy.start()
    return copy


def camera_columns(cameras_ref):
    return [cameras_ref[:, at : at + 1] for at in range(6)]


def sigmoid(value):
    return 1.0 / (1.0 + jnp.exp(-value))


def fold(value):
    return value[0:8] + value[8:16]


def wide(row):
    eight = jnp.broadcast_to(row, (8, row.shape[1]))
    return jnp.concatenate([eight, eight], axis=0)


def step_kernel(
    width,
    height,
    lengths_ref,
    cameras_ref,
    params_ref,
    lists_ref,
    target_ref,
    out_ref,
    rows_ref,
    table_ref,
    dense_ref,
    landing_ref,
    summed_ref,
    view_send,
    view_recv,
    tile_send,
    tile_recv,
    view_send_back,
    view_recv_back,
    tile_send_back,
    tile_recv_back,
    picked,
    keeps,
    suffix,
    before,
    after,
    alpha_s,
    ratio_s,
    flow_s,
    chosen,
    one_hot,
    spread,
):
    f32, bf16 = jnp.float32, jnp.bfloat16
    tile_dev, list_size = lists_ref.shape
    tile_groups, view_count, _, owned = table_ref.shape
    per_owner = owned // 128
    halves = list_size // 128
    views = rotated(lax.axis_index("views"), view_count)
    tiles = rotated(lax.axis_index("tiles"), tile_groups)
    everyone_here = greet(views, tiles)
    values = [params_ref[at : at + 1, :] for at in range(59)]
    made = project(
        values, camera_columns(cameras_ref), float(width), 0.5 * width, 0.5 * height
    )
    opacities = jnp.broadcast_to(sigmoid(values[10]), (view_count, owned))
    for row_at, value in enumerate(made[:5] + (opacities,) + made[5:]):
        rows_ref[:, row_at, :] = value
    everyone_here()
    mine = table_ref.at[tiles[0]]
    over_views = [
        send(
            rows_ref.at[view],
            mine.at[views[0]],
            view_send.at[at],
            view_recv.at[at],
            (view, tiles[0]),
        )
        for at, view in enumerate(views[1:])
    ]
    table_ref[pl.ds(tiles[0], 1), pl.ds(views[0], 1)] = rows_ref[pl.ds(views[0], 1)][None]
    for copy in over_views:
        copy.wait()
    over_tiles = [
        send(mine, mine, tile_send.at[at], tile_recv.at[at], (views[0], tile))
        for at, tile in enumerate(tiles[1:])
    ]

    row_ids = lax.broadcasted_iota(jnp.int32, (list_size, list_size), 0)
    col_ids = lax.broadcasted_iota(jnp.int32, (list_size, list_size), 1)
    for piece in range(2):
        here = slice(piece * list_size, (piece + 1) * list_size)
        before[here, :] = (row_ids < col_ids).astype(f32).astype(bf16)
        after[here, :] = (row_ids > col_ids).astype(f32).astype(bf16)
    spread[...] = jnp.zeros_like(spread)
    lane_ids = lax.broadcasted_iota(jnp.int32, (1, list_size), 1)
    pixel_ids = lax.broadcasted_iota(jnp.int32, (16, list_size), 0).astype(f32)
    column_ids = lax.broadcasted_iota(jnp.int32, (256, list_size), 0)
    first_tile = tiles[0] * tile_dev
    entries = lists_ref[...]
    block_of = entries >> 7
    column_of = entries & 127

    def gather_from(tile_group, carry):
        carry = list(carry)
        for view in range(view_count):
            for part in range(per_owner):
                lanes = slice(part * 128, part * 128 + 128)
                block = (view * tile_groups + tile_group) * per_owner + part
                for half in range(halves):
                    here = slice(half * 128, half * 128 + 128)
                    mask = block_of[:, here] == block
                    column = column_of[:, here]
                    for row_at in range(9):
                        line = table_ref[tile_group, view, row_at : row_at + 1, lanes]
                        got = jnp.take_along_axis(
                            jnp.broadcast_to(line, (tile_dev, 128)),
                            column,
                            axis=1,
                            mode="promise_in_bounds",
                        )
                        slot = half * 9 + row_at
                        carry[slot] = jnp.where(mask, got, carry[slot])
        return tuple(carry)

    def gather_arrived(at, carry):
        source = lax.rem(tiles[0] + tile_groups - at, tile_groups)
        pltpu.make_async_remote_copy(
            src_ref=mine,
            dst_ref=table_ref.at[source],
            send_sem=tile_send.at[at - 1],
            recv_sem=tile_recv.at[at - 1],
            device_id=(views[0], source),
            device_id_type=pl.DeviceIdType.MESH,
        ).wait_recv()
        return gather_from(source, carry)

    gathered = tuple(jnp.zeros((tile_dev, 128), f32) for _ in range(halves * 9))
    gathered = gather_from(tiles[0], gathered)
    gathered = lax.fori_loop(1, tile_groups, gather_arrived, gathered)
    for half in range(halves):
        for row_at in range(9):
            picked[row_at, :, half * 128 : half * 128 + 128] = gathered[half * 9 + row_at]
    for copy in over_tiles:
        copy.wait_send()
    group = spread.shape[1] // 32
    pair = keeps.shape[0]
    lines = [slice(line * 16, line * 16 + 16) for line in range(TILE_SIDE)]

    def load_tile(tile_at):
        tile_id = first_tile + tile_at
        left = (tile_id % TILE_COLS * TILE_SIDE).astype(f32) + 0.5
        top = (tile_id // TILE_COLS * TILE_SIDE).astype(f32) + 0.5
        rows = [picked[row_at, pl.ds(tile_at, 1), :] for row_at in range(9)]
        rows[5] = jnp.where(lane_ids < lengths_ref[tile_at], rows[5], 0.0)
        delta_x = (pixel_ids + left) - wide(rows[0])
        return rows, delta_x, top

    def delta_y_at(rows, top, line):
        return (top + float(line)) - wide(rows[1])

    def alphas_of(slot, rows, delta_x, top):
        opacity = wide(rows[5])
        part_a = wide(-0.5 * rows[2]) * delta_x * delta_x
        part_b = wide(-rows[3]) * delta_x
        half_c = wide(-0.5 * rows[4])
        for line, here in enumerate(lines):
            delta_y = delta_y_at(rows, top, line)
            alphas = opacity * jnp.exp(part_a + delta_y * (part_b + half_c * delta_y))
            log_keep = jnp.log(1.0 - alphas)
            high = log_keep.astype(bf16)
            keeps[slot, here, 0:list_size] = high
            keeps[slot, here, list_size : 2 * list_size] = (log_keep - high.astype(f32)).astype(bf16)
            alpha_s[slot, here, :] = alphas
            ratio_s[slot, here, :] = alphas * jnp.exp(-log_keep)

    def weights_of(slot, tile_at, rows, passed):
        wanted = jnp.concatenate(
            [target_ref[channel, pl.ds(tile_at, 1), :] for channel in range(3)]
            + [jnp.zeros((5, TILE_SIDE * TILE_SIDE), f32)],
            axis=0,
        ).T
        colors = [wide(row) for row in rows[6:9]]
        color_sums = [jnp.zeros((8, list_size), f32) for _ in range(3)]
        for here in lines:
            weight = jnp.exp(passed[here]) * alpha_s[slot, here, :]
            flow = None
            for channel, color in enumerate(colors):
                colored = weight * color
                gap = jnp.sum(colored, axis=1, keepdims=True) - wanted[here, channel : channel + 1]
                sign = jnp.where(gap > 0.0, 1.0, jnp.where(gap < 0.0, -1.0, 0.0))
                sign = jnp.broadcast_to(sign, colored.shape)
                color_sums[channel] = color_sums[channel] + fold(weight * sign)
                flow = colored * sign if flow is None else flow + colored * sign
            high = flow.astype(bf16)
            suffix[slot, here, 0:list_size] = high
            suffix[slot, here, list_size : 2 * list_size] = (flow - high.astype(f32)).astype(bf16)
            flow_s[slot, here, :] = flow
        return color_sums

    def grads_of(slot, rows, delta_x, top, behind, color_sums):
        sums = [jnp.zeros((8, list_size), f32) for _ in range(6)]
        for line, here in enumerate(lines):
            delta_y = delta_y_at(rows, top, line)[0:8]
            pull = flow_s[slot, here, :] - behind[here] * ratio_s[slot, here, :]
            pull_x = pull * delta_x
            pull_xx = fold(pull_x * delta_x)
            pull_x = fold(pull_x)
            pull = fold(pull)
            pull_y = pull * delta_y
            terms = (pull, pull_x, pull_y, pull_xx, pull_x * delta_y, pull_y * delta_y)
            sums = [total + term for total, term in zip(sums, terms)]
        flat, by_x, by_y, by_xx, by_xy, by_yy = [
            jnp.sum(total, axis=0, keepdims=True) for total in sums
        ]
        _, _, con_a, con_b, con_c = rows[:5]
        return jnp.concatenate(
            [
                con_a * by_x + con_b * by_y,
                con_b * by_x + con_c * by_y,
                -0.5 * by_xx,
                -by_xy,
                -0.5 * by_yy,
                flat,
            ]
            + [jnp.sum(total, axis=0, keepdims=True) for total in color_sums]
            + [jnp.zeros((7, list_size), f32)],
            axis=0,
        )

    def some_tiles(step, carry):
        slots = range(pair)
        at = [step * pair + slot for slot in slots]
        tiles = [load_tile(tile_at) for tile_at in at]
        for slot in slots:
            alphas_of(slot, *tiles[slot])
        passed = [jnp.dot(keeps[slot], before[...], preferred_element_type=f32) for slot in slots]
        color_sums = [weights_of(slot, at[slot], tiles[slot][0], passed[slot]) for slot in slots]
        behind = [jnp.dot(suffix[slot], after[...], preferred_element_type=f32) for slot in slots]
        owners, pieces = [], []
        for slot in slots:
            grads = grads_of(slot, *tiles[slot], behind[slot], color_sums[slot])
            high = grads.astype(bf16).astype(f32)
            pieces.append(jnp.concatenate([high, grads - high], axis=0))
            ids = lists_ref[pl.ds(at[slot], 1), :]
            owners.append(wide(ids >> 8))
            lanes = slice(slot * list_size, (slot + 1) * list_size)
            one_hot[:, lanes] = (column_ids == (ids & 255)).astype(f32).astype(bf16)

        def spread_group(group_at, carry):
            for slot in slots:
                lanes = slice(slot * list_size, (slot + 1) * list_size)
                for block in range(group):
                    mask = owners[slot] == group_at * group + block
                    mask = jnp.concatenate([mask, mask], axis=0)
                    chosen[block * 32 : block * 32 + 32, lanes] = jnp.where(
                        mask, pieces[slot], 0.0
                    ).astype(bf16)
            spread[group_at] += lax.dot_general(
                chosen[...], one_hot[...], (((1,), (1,)), ((), ())), preferred_element_type=f32
            )
            return carry

        if spread.shape[0] == 1:
            spread_group(0, 0)
        else:
            lax.fori_loop(0, spread.shape[0], spread_group, 0)
        return carry

    lax.fori_loop(0, tile_dev // pair, some_tiles, 0)

    def finish_group(group_at, carry):
        for block in range(group):
            both = spread[group_at, block * 32 : block * 32 + 32, :]
            total = both[0:16] + both[16:32]
            for half in range(2):
                chunk = block * 2 + half
                owner = group_at * (2 * group // per_owner) + chunk // per_owner
                lanes = chunk % per_owner * 128
                dense_ref[owner % tile_groups, owner // tile_groups, :, lanes : lanes + 128] = total[
                    0:9, half * 128 : half * 128 + 128
                ]
        return carry

    if spread.shape[0] == 1:
        finish_group(0, 0)
    else:
        lax.fori_loop(0, spread.shape[0], finish_group, 0)

    over_tiles = [
        send(
            dense_ref.at[tile],
            landing_ref.at[at],
            tile_send_back.at[at],
            tile_recv_back.at[at],
            (views[0], tile),
        )
        for at, tile in enumerate(tiles[1:])
    ]
    total = dense_ref[pl.ds(tiles[0], 1)][0]
    for at, copy in enumerate(over_tiles):
        copy.wait()
        total = total + landing_ref[at]
    summed_ref[...] = total
    over_views = [
        send(
            summed_ref.at[view],
            out_ref.at[views[0]],
            view_send_back.at[at],
            view_recv_back.at[at],
            (view, tiles[0]),
        )
        for at, view in enumerate(views[1:])
    ]
    out_ref[pl.ds(views[0], 1)] = summed_ref[pl.ds(views[0], 1)]
    for copy in over_views:
        copy.wait()


def update_kernel(
    width,
    height,
    cameras_ref,
    rates_ref,
    grads_ref,
    params_ref,
    first_ref,
    second_ref,
    new_params_ref,
    new_first_ref,
    new_second_ref,
):
    camera = camera_columns(cameras_ref)
    values = [params_ref[at : at + 1, :] for at in range(59)]
    _, pullback = jax.vjp(
        lambda rows: project(rows, camera, float(width), 0.5 * width, 0.5 * height), values
    )
    given = [grads_ref[:, row_at, :] for row_at in range(9)]
    grads = list(pullback(tuple(given[:5] + given[6:]))[0])
    grads[10] = jnp.sum(given[5], axis=0, keepdims=True) * (1.0 - sigmoid(values[10]))
    for at in range(59):
        new_first_ref[at : at + 1, :] = grads[at]
    gradient = new_first_ref[...]
    new_first = beta_one * first_ref[...] + (1.0 - beta_one) * gradient
    new_second = beta_two * second_ref[...] + (1.0 - beta_two) * gradient * gradient
    new_first_ref[...] = new_first
    new_second_ref[...] = new_second
    step_size = rates_ref[...] * (new_first / (1.0 - beta_one**ADAM_STEP))
    new_params_ref[...] = params_ref[...] - step_size / (
        jnp.sqrt(new_second / (1.0 - beta_two**ADAM_STEP)) + adam_eps
    )


def in_vmem(count):
    return [pl.BlockSpec(memory_space=pltpu.VMEM)] * count


def per_device(params, first_moment, second_moment, cameras, target, lists, lengths):
    f32, bf16 = jnp.float32, jnp.bfloat16
    view_count = lax.axis_size("views")
    tile_groups = lax.axis_size("tiles")
    peers = view_count * tile_groups
    owned = params.shape[1]
    tile_dev = target.shape[1]
    list_size = lists.shape[2]
    pixels = target.shape[3]
    width = TILE_COLS * TILE_SIDE
    height = tile_dev * tile_groups // TILE_COLS * TILE_SIDE
    limit = 40 * 1024 * 1024

    dma = pltpu.SemaphoreType.DMA
    semaphores = [
        dma((view_count,)),
        dma((view_count,)),
        dma((tile_groups,)),
        dma((tile_groups,)),
    ]
    by_owner = (tile_groups, view_count, 9, owned)
    block_rows = (view_count, 9, owned)
    blocks = peers * owned // 256
    group = 16
    pair = 2
    row_grads = pl.pallas_call(
        lambda *refs: step_kernel(width, height, *refs),
        out_shape=jax.ShapeDtypeStruct(block_rows, f32),
        in_specs=[pl.BlockSpec(memory_space=pltpu.SMEM)] + in_vmem(4),
        out_specs=pl.BlockSpec(memory_space=pltpu.VMEM),
        scratch_shapes=[
            pltpu.VMEM(block_rows, f32),
            pltpu.VMEM(by_owner, f32),
            pltpu.VMEM(by_owner, f32),
            pltpu.VMEM((tile_groups - 1,) + block_rows, f32),
            pltpu.VMEM(block_rows, f32),
        ]
        + semaphores
        + semaphores
        + [
            pltpu.VMEM((9, tile_dev, list_size), f32),
            pltpu.VMEM((pair, pixels, 2 * list_size), bf16),
            pltpu.VMEM((pair, pixels, 2 * list_size), bf16),
            pltpu.VMEM((2 * list_size, list_size), bf16),
            pltpu.VMEM((2 * list_size, list_size), bf16),
            pltpu.VMEM((pair, pixels, list_size), f32),
            pltpu.VMEM((pair, pixels, list_size), f32),
            pltpu.VMEM((pair, pixels, list_size), f32),
            pltpu.VMEM((group * 32, pair * list_size), bf16),
            pltpu.VMEM((256, pair * list_size), bf16),
            pltpu.VMEM((blocks // group, group * 32, 256), f32),
        ],
        compiler_params=pltpu.CompilerParams(
            collective_id=0, has_side_effects=True, vmem_limit_bytes=limit
        ),
        name="splat_gradients",
    )(lengths[0], cameras, params, lists[0], target[0].transpose(1, 0, 2))

    like = jax.ShapeDtypeStruct(params.shape, f32)
    return pl.pallas_call(
        lambda *refs: update_kernel(width, height, *refs),
        out_shape=(like, like, like),
        in_specs=in_vmem(6),
        out_specs=tuple(in_vmem(3)),
        compiler_params=pltpu.CompilerParams(vmem_limit_bytes=limit // 4),
        name="update_gaussians",
    )(cameras, jnp.asarray(learning), row_grads, params, first_moment, second_moment)


def solution(mesh):
    placed = (
        P(None, ("views", "tiles")),
        P(None, ("views", "tiles")),
        P(None, ("views", "tiles")),
        P(),
        P("views", "tiles", None, None),
        P("views", "tiles", None),
        P("views", "tiles"),
    )
    return jax.shard_map(
        per_device,
        mesh=mesh,
        in_specs=placed,
        out_specs=(
            P(None, ("views", "tiles")),
            P(None, ("views", "tiles")),
            P(None, ("views", "tiles")),
        ),
        check_vma=False,
    )
```

```python
import jax
import jax.numpy as jnp
import numpy as np
from jax import lax
from jax.experimental import pallas as pl
from jax.experimental.pallas import tpu as pltpu
from jax.sharding import PartitionSpec as P

TILE_SIDE = 16
TILE_COLS = 32
ADAM_STEP = 1000


sh_zero = 0.28209479177387814
sh_first = 0.4886025119029199
sh_second = (
    1.0925484305920792,
    -1.0925484305920792,
    0.31539156525252005,
    -1.0925484305920792,
    0.5462742152960396,
)
sh_third = (
    -0.5900435899266435,
    2.890611442640554,
    -0.4570457994644658,
    0.3731763325901154,
    -0.4570457994644658,
    1.445305721320277,
    -0.5900435899266435,
)
beta_one = 0.9
beta_two = 0.999
adam_eps = 1e-15
learning = np.concatenate(
    [
        np.full(3, 0.00016),
        np.full(3, 0.005),
        np.full(4, 0.001),
        np.full(1, 0.05),
        np.full(3, 0.0025),
        np.full(45, 0.000125),
    ]
).astype(np.float32)[:, None]


def matmul_three(left, right):
    return [
        [
            left[row_at][0] * right[0][col_at]
            + left[row_at][1] * right[1][col_at]
            + left[row_at][2] * right[2][col_at]
            for col_at in range(3)
        ]
        for row_at in range(3)
    ]


def camera_rotation(camera):
    cos_a, sin_a = (jnp.cos(camera[0]), jnp.sin(camera[0]))
    cos_b, sin_b = (jnp.cos(camera[1]), jnp.sin(camera[1]))
    cos_c, sin_c = (jnp.cos(camera[2]), jnp.sin(camera[2]))
    around_x = [[1.0, 0.0, 0.0], [0.0, cos_a, -sin_a], [0.0, sin_a, cos_a]]
    around_y = [[cos_b, 0.0, sin_b], [0.0, 1.0, 0.0], [-sin_b, 0.0, cos_b]]
    around_z = [[cos_c, -sin_c, 0.0], [sin_c, cos_c, 0.0], [0.0, 0.0, 1.0]]
    return matmul_three(around_z, matmul_three(around_y, around_x))


def sh_basis(along_x, along_y, along_z):
    square_x, square_y, square_z = (along_x * along_x, along_y * along_y, along_z * along_z)
    both_xy, both_yz, both_xz = (along_x * along_y, along_y * along_z, along_x * along_z)
    return [
        sh_zero + 0.0 * along_x,
        -sh_first * along_y,
        sh_first * along_z,
        -sh_first * along_x,
        sh_second[0] * both_xy,
        sh_second[1] * both_yz,
        sh_second[2] * (2.0 * square_z - square_x - square_y),
        sh_second[3] * both_xz,
        sh_second[4] * (square_x - square_y),
        sh_third[0] * along_y * (3.0 * square_x - square_y),
        sh_third[1] * both_xy * along_z,
        sh_third[2] * along_y * (4.0 * square_z - square_x - square_y),
        sh_third[3] * along_z * (2.0 * square_z - 3.0 * square_x - 3.0 * square_y),
        sh_third[4] * along_x * (4.0 * square_z - square_x - square_y),
        sh_third[5] * along_z * (square_x - square_y),
        sh_third[6] * along_x * (square_x - 3.0 * square_y),
    ]


def project(rows, camera, focal_len, center_x, center_y):
    rotation = camera_rotation(camera)
    means = rows[0:3]
    point = [
        rotation[axis_at][0] * means[0]
        + rotation[axis_at][1] * means[1]
        + rotation[axis_at][2] * means[2]
        + camera[3 + axis_at]
        for axis_at in range(3)
    ]
    inverse_z = 1.0 / point[2]
    screen_u = focal_len * point[0] * inverse_z + center_x
    screen_v = focal_len * point[1] * inverse_z + center_y
    scales = [jnp.exp(value) for value in rows[3:6]]
    norm = rows[6] * rows[6] + rows[7] * rows[7] + rows[8] * rows[8] + rows[9] * rows[9]
    inverse_norm = lax.rsqrt(norm)
    real_part, imag_x, imag_y, imag_z = [value * inverse_norm for value in rows[6:10]]
    spin = [
        [
            1.0 - 2.0 * (imag_y * imag_y + imag_z * imag_z),
            2.0 * (imag_x * imag_y - real_part * imag_z),
            2.0 * (imag_x * imag_z + real_part * imag_y),
        ],
        [
            2.0 * (imag_x * imag_y + real_part * imag_z),
            1.0 - 2.0 * (imag_x * imag_x + imag_z * imag_z),
            2.0 * (imag_y * imag_z - real_part * imag_x),
        ],
        [
            2.0 * (imag_x * imag_z - real_part * imag_y),
            2.0 * (imag_y * imag_z + real_part * imag_x),
            1.0 - 2.0 * (imag_x * imag_x + imag_y * imag_y),
        ],
    ]
    turned = matmul_three(rotation, spin)
    shaped = [
        [turned[row_at][col_at] * scales[col_at] for col_at in range(3)] for row_at in range(3)
    ]
    near_x = [
        focal_len * inverse_z * shaped[0][col_at]
        - focal_len * point[0] * inverse_z * inverse_z * shaped[2][col_at]
        for col_at in range(3)
    ]
    near_y = [
        focal_len * inverse_z * shaped[1][col_at]
        - focal_len * point[1] * inverse_z * inverse_z * shaped[2][col_at]
        for col_at in range(3)
    ]
    cov_a = near_x[0] * near_x[0] + near_x[1] * near_x[1] + near_x[2] * near_x[2] + 0.3
    cov_b = near_x[0] * near_y[0] + near_x[1] * near_y[1] + near_x[2] * near_y[2]
    cov_c = near_y[0] * near_y[0] + near_y[1] * near_y[1] + near_y[2] * near_y[2] + 0.3
    determinant = cov_a * cov_c - cov_b * cov_b
    offset = [
        means[axis_at]
        + rotation[0][axis_at] * camera[3]
        + rotation[1][axis_at] * camera[4]
        + rotation[2][axis_at] * camera[5]
        for axis_at in range(3)
    ]
    inverse_len = lax.rsqrt(offset[0] * offset[0] + offset[1] * offset[1] + offset[2] * offset[2])
    basis = sh_basis(offset[0] * inverse_len, offset[1] * inverse_len, offset[2] * inverse_len)
    colors = [
        0.5 + sum((basis[coef_at] * rows[11 + 3 * coef_at + channel] for coef_at in range(16)))
        for channel in range(3)
    ]
    return (
        screen_u,
        screen_v,
        cov_c / determinant,
        -cov_b / determinant,
        cov_a / determinant,
        colors[0],
        colors[1],
        colors[2],
    )


def rotated(start, count):
    return [lax.rem(start + step, count) for step in range(count)]


def greet(views, tiles):
    barrier = pltpu.get_barrier_semaphore()
    here = (views[0], tiles[0])
    others = [(view, here[1]) for view in views[1:]] + [(here[0], tile) for tile in tiles[1:]]
    for device in others:
        pl.semaphore_signal(
            barrier, inc=1, device_id=device, device_id_type=pl.DeviceIdType.MESH
        )
    return lambda: pl.semaphore_wait(barrier, len(others))


def send(source, landing, send_sem, recv_sem, device):
    copy = pltpu.make_async_remote_copy(
        src_ref=source,
        dst_ref=landing,
        send_sem=send_sem,
        recv_sem=recv_sem,
        device_id=device,
        device_id_type=pl.DeviceIdType.MESH,
    )
    copy.start()
    return copy


def camera_columns(cameras_ref):
    return [cameras_ref[:, at : at + 1] for at in range(6)]


def sigmoid(value):
    return 1.0 / (1.0 + jnp.exp(-value))


def fold(value):
    return value[0:8] + value[8:16]


def wide(row):
    eight = jnp.broadcast_to(row, (8, row.shape[1]))
    return jnp.concatenate([eight, eight], axis=0)


def step_kernel(
    width,
    height,
    lengths_ref,
    cameras_far,
    params_far,
    lists_far,
    target_far,
    out_ref,
    cameras_ref,
    params_ref,
    lists_ref,
    target_ref,
    fetch_sem,
    rows_ref,
    table_ref,
    dense_ref,
    landing_ref,
    summed_ref,
    view_send,
    view_recv,
    tile_send,
    tile_recv,
    view_send_back,
    view_recv_back,
    tile_send_back,
    tile_recv_back,
    picked,
    keeps,
    suffix,
    before,
    after,
    alpha_s,
    ratio_s,
    flow_s,
    weight_s,
    painted,
    paints,
    tints,
    chosen,
    one_hot,
    spread,
):
    f32, bf16 = jnp.float32, jnp.bfloat16
    tile_dev, list_size = lists_ref.shape
    tile_groups, view_count, _, owned = table_ref.shape
    per_owner = owned // 128
    halves = list_size // 128
    views = rotated(lax.axis_index("views"), view_count)
    tiles = rotated(lax.axis_index("tiles"), tile_groups)
    pairs = ((params_far, params_ref), (cameras_far, cameras_ref))
    pairs = pairs + ((lists_far, lists_ref), (target_far, target_ref))
    fetches = [
        pltpu.make_async_copy(far, near, fetch_sem.at[at]) for at, (far, near) in enumerate(pairs)
    ]
    for fetch in fetches:
        fetch.start()
    everyone_here = greet(views, tiles)
    for fetch in fetches[:2]:
        fetch.wait()
    values = [params_ref[at : at + 1, :] for at in range(59)]
    made = project(
        values, camera_columns(cameras_ref), float(width), 0.5 * width, 0.5 * height
    )
    opacities = jnp.broadcast_to(sigmoid(values[10]), (view_count, owned))
    for row_at, value in enumerate(made[:5] + (opacities,) + made[5:]):
        rows_ref[:, row_at, :] = value
    everyone_here()
    mine = table_ref.at[tiles[0]]
    over_views = [
        send(
            rows_ref.at[view],
            mine.at[views[0]],
            view_send.at[at],
            view_recv.at[at],
            (view, tiles[0]),
        )
        for at, view in enumerate(views[1:])
    ]
    table_ref[pl.ds(tiles[0], 1), pl.ds(views[0], 1)] = rows_ref[pl.ds(views[0], 1)][None]
    for copy in over_views:
        copy.wait()
    over_tiles = [
        send(mine, mine, tile_send.at[at], tile_recv.at[at], (views[0], tile))
        for at, tile in enumerate(tiles[1:])
    ]

    row_ids = lax.broadcasted_iota(jnp.int32, (list_size, list_size), 0)
    col_ids = lax.broadcasted_iota(jnp.int32, (list_size, list_size), 1)
    for piece in range(2):
        here = slice(piece * list_size, (piece + 1) * list_size)
        before[here, :] = (row_ids < col_ids).astype(f32).astype(bf16)
        after[here, :] = (row_ids > col_ids).astype(f32).astype(bf16)
    spread[...] = jnp.zeros_like(spread)
    tints[...] = jnp.zeros_like(tints)
    paints[...] = jnp.zeros_like(paints)
    painted[:, :, 3 * list_size :] = jnp.zeros(
        (painted.shape[0], painted.shape[1], 128), bf16
    )
    channels = lax.broadcasted_iota(jnp.int32, (16, 128), 0)
    pieces_at = lax.broadcasted_iota(jnp.int32, (16, 128), 1)
    same = (channels % 3 == pieces_at % 3) & (channels < 9) & (pieces_at < 9)
    for slot in range(paints.shape[0]):
        paints[slot, 0:16, 3 * list_size :] = jnp.where(same, -1.0, 0.0).astype(bf16)
    lane_ids = lax.broadcasted_iota(jnp.int32, (1, list_size), 1)
    pixel_ids = lax.broadcasted_iota(jnp.int32, (16, list_size), 0).astype(f32)
    column_ids = lax.broadcasted_iota(jnp.int32, (256, list_size), 0)
    first_tile = tiles[0] * tile_dev
    for fetch in fetches[2:]:
        fetch.wait()
    entries = lists_ref[...]
    block_of = entries >> 7
    column_of = entries & 127

    def gather_from(tile_group, carry):
        carry = list(carry)
        for view in range(view_count):
            for part in range(per_owner):
                lanes = slice(part * 128, part * 128 + 128)
                block = (view * tile_groups + tile_group) * per_owner + part
                for half in range(halves):
                    here = slice(half * 128, half * 128 + 128)
                    mask = block_of[:, here] == block
                    column = column_of[:, here]
                    for row_at in range(9):
                        line = table_ref[tile_group, view, row_at : row_at + 1, lanes]
                        got = jnp.take_along_axis(
                            jnp.broadcast_to(line, (tile_dev, 128)),
                            column,
                            axis=1,
                            mode="promise_in_bounds",
                        )
                        slot = half * 9 + row_at
                        carry[slot] = jnp.where(mask, got, carry[slot])
        return tuple(carry)

    def gather_arrived(at, carry):
        source = lax.rem(tiles[0] + tile_groups - at, tile_groups)
        pltpu.make_async_remote_copy(
            src_ref=mine,
            dst_ref=table_ref.at[source],
            send_sem=tile_send.at[at - 1],
            recv_sem=tile_recv.at[at - 1],
            device_id=(views[0], source),
            device_id_type=pl.DeviceIdType.MESH,
        ).wait_recv()
        return gather_from(source, carry)

    gathered = tuple(jnp.zeros((tile_dev, 128), f32) for _ in range(halves * 9))
    gathered = gather_from(tiles[0], gathered)
    gathered = lax.fori_loop(1, tile_groups, gather_arrived, gathered)
    for half in range(halves):
        for row_at in range(9):
            picked[row_at, :, half * 128 : half * 128 + 128] = gathered[half * 9 + row_at]
    for copy in over_tiles:
        copy.wait_send()
    group = spread.shape[1] // 32
    pair = keeps.shape[0]
    lines = [slice(line * 16, line * 16 + 16) for line in range(TILE_SIDE)]

    def load_tile(tile_at):
        tile_id = first_tile + tile_at
        left = (tile_id % TILE_COLS * TILE_SIDE).astype(f32) + 0.5
        top = (tile_id // TILE_COLS * TILE_SIDE).astype(f32) + 0.5
        rows = [picked[row_at, pl.ds(tile_at, 1), :] for row_at in range(9)]
        rows[5] = jnp.where(lane_ids < lengths_ref[tile_at], rows[5], 0.0)
        delta_x = (pixel_ids + left) - wide(rows[0])
        return rows, delta_x, top

    def delta_y_at(rows, top, line):
        return (top + float(line)) - wide(rows[1])

    def alphas_of(slot, rows, delta_x, top):
        opacity = wide(rows[5])
        part_a = wide(-0.5 * rows[2]) * delta_x * delta_x
        part_b = wide(-rows[3]) * delta_x
        half_c = wide(-0.5 * rows[4])
        for line, here in enumerate(lines):
            delta_y = delta_y_at(rows, top, line)
            alphas = opacity * jnp.exp(part_a + delta_y * (part_b + half_c * delta_y))
            log_keep = jnp.log(1.0 - alphas)
            high = log_keep.astype(bf16)
            keeps[slot, here, 0:list_size] = high
            keeps[slot, here, list_size : 2 * list_size] = (log_keep - high.astype(f32)).astype(bf16)
            alpha_s[slot, here, :] = alphas
            ratio_s[slot, here, :] = alphas * jnp.exp(-log_keep)

    def split(value):
        high = value.astype(bf16)
        return high, (value - high.astype(f32)).astype(bf16)

    def colors_of(slot, tile_at, rows):
        empty = jnp.zeros((7, list_size), f32)
        colors = jnp.concatenate(rows[6:9], axis=0)
        high = colors.astype(bf16).astype(f32)
        middle = (colors - high).astype(bf16).astype(f32)
        low = colors - high - middle
        highs = jnp.concatenate([high, high, high, empty], axis=0).astype(bf16)
        lows = jnp.concatenate([middle, middle, middle, empty], axis=0).astype(bf16)
        paints[slot, 0:16, 0:list_size] = highs
        paints[slot, 0:16, list_size : 2 * list_size] = highs
        paints[slot, 0:16, 2 * list_size : 3 * list_size] = lows
        tints[slot, 0:16, :] = jnp.concatenate([high, middle, low, empty], axis=0).astype(bf16)
        wanted = jnp.concatenate(
            [target_ref[channel, pl.ds(tile_at, 1), :] for channel in range(3)], axis=0
        )
        high = wanted.astype(bf16).astype(f32)
        middle = (wanted - high).astype(bf16).astype(f32)
        low = wanted - high - middle
        wanted = jnp.concatenate([high, middle, low, jnp.zeros((7, wanted.shape[1]), f32)], axis=0)
        painted[slot, :, 3 * list_size : 3 * list_size + 16] = wanted.T.astype(bf16)

    def weights_of(slot, passed):
        for here in lines:
            weight = jnp.exp(passed[here]) * alpha_s[slot, here, :]
            high, low = split(weight)
            weight_s[slot, here, :] = weight
            painted[slot, here, 0:list_size] = high
            painted[slot, here, list_size : 2 * list_size] = low
            painted[slot, here, 2 * list_size : 3 * list_size] = high

    def signs_of(gaps):
        return jnp.where(gaps > 0.0, 1.0, jnp.where(gaps < 0.0, -1.0, 0.0))

    def color_grads(slot, signs):
        turned = signs.T[0:16].astype(bf16)
        both = jnp.dot(turned, painted[slot, :, 0 : 2 * list_size], preferred_element_type=f32)
        return both[0:3, 0:list_size] + both[0:3, list_size : 2 * list_size]

    def flows_of(slot, tinted):
        for here in lines:
            flow = weight_s[slot, here, :] * tinted[here]
            high, low = split(flow)
            suffix[slot, here, 0:list_size] = high
            suffix[slot, here, list_size : 2 * list_size] = low
            flow_s[slot, here, :] = flow

    def grads_of(slot, rows, delta_x, top, behind, color_sums):
        sums = [jnp.zeros((8, list_size), f32) for _ in range(6)]
        for line, here in enumerate(lines):
            delta_y = delta_y_at(rows, top, line)[0:8]
            pull = flow_s[slot, here, :] - behind[here] * ratio_s[slot, here, :]
            pull_x = pull * delta_x
            pull_xx = fold(pull_x * delta_x)
            pull_x = fold(pull_x)
            pull = fold(pull)
            pull_y = pull * delta_y
            terms = (pull, pull_x, pull_y, pull_xx, pull_x * delta_y, pull_y * delta_y)
            sums = [total + term for total, term in zip(sums, terms)]
        flat, by_x, by_y, by_xx, by_xy, by_yy = [
            jnp.sum(total, axis=0, keepdims=True) for total in sums
        ]
        _, _, con_a, con_b, con_c = rows[:5]
        return jnp.concatenate(
            [
                con_a * by_x + con_b * by_y,
                con_b * by_x + con_c * by_y,
                -0.5 * by_xx,
                -by_xy,
                -0.5 * by_yy,
                flat,
            ]
            + [color_sums]
            + [jnp.zeros((7, list_size), f32)],
            axis=0,
        )

    def some_tiles(step, carry):
        slots = range(pair)
        at = [step * pair + slot for slot in slots]
        arrived = [load_tile(tile_at) for tile_at in at]
        passed, gaps, tinted, color_sums, behind = [], [], [], [], []
        for slot in slots:
            alphas_of(slot, *arrived[slot])
            passed.append(jnp.dot(keeps[slot], before[...], preferred_element_type=f32))
            colors_of(slot, at[slot], arrived[slot][0])
        for slot in slots:
            weights_of(slot, passed[slot])
            gaps.append(
                lax.dot_general(
                    painted[slot], paints[slot], (((1,), (1,)), ((), ())), preferred_element_type=f32
                )
            )
        for slot in slots:
            signs = signs_of(gaps[slot])
            tinted.append(jnp.dot(signs.astype(bf16), tints[slot], preferred_element_type=f32))
            color_sums.append(color_grads(slot, signs))
        for slot in slots:
            flows_of(slot, tinted[slot])
            behind.append(jnp.dot(suffix[slot], after[...], preferred_element_type=f32))
        owners, pieces = [], []
        for slot in slots:
            grads = grads_of(slot, *arrived[slot], behind[slot], color_sums[slot])
            high = grads.astype(bf16).astype(f32)
            pieces.append(jnp.concatenate([high, grads - high], axis=0))
            ids = lists_ref[pl.ds(at[slot], 1), :]
            owners.append(wide(ids >> 8))
            lanes = slice(slot * list_size, (slot + 1) * list_size)
            one_hot[:, lanes] = (column_ids == (ids & 255)).astype(f32).astype(bf16)

        def spread_group(group_at, carry):
            for slot in slots:
                lanes = slice(slot * list_size, (slot + 1) * list_size)
                for block in range(group):
                    mask = owners[slot] == group_at * group + block
                    mask = jnp.concatenate([mask, mask], axis=0)
                    chosen[block * 32 : block * 32 + 32, lanes] = jnp.where(
                        mask, pieces[slot], 0.0
                    ).astype(bf16)
            spread[group_at] += lax.dot_general(
                chosen[...], one_hot[...], (((1,), (1,)), ((), ())), preferred_element_type=f32
            )
            return carry

        if spread.shape[0] == 1:
            spread_group(0, 0)
        else:
            lax.fori_loop(0, spread.shape[0], spread_group, 0)
        return carry

    lax.fori_loop(0, tile_dev // pair, some_tiles, 0)

    def finish_group(group_at, carry):
        for block in range(group):
            both = spread[group_at, block * 32 : block * 32 + 32, :]
            total = both[0:16] + both[16:32]
            for half in range(2):
                chunk = block * 2 + half
                owner = group_at * (2 * group // per_owner) + chunk // per_owner
                lanes = chunk % per_owner * 128
                dense_ref[owner % tile_groups, owner // tile_groups, :, lanes : lanes + 128] = total[
                    0:9, half * 128 : half * 128 + 128
                ]
        return carry

    if spread.shape[0] == 1:
        finish_group(0, 0)
    else:
        lax.fori_loop(0, spread.shape[0], finish_group, 0)

    over_tiles = [
        send(
            dense_ref.at[tile],
            landing_ref.at[at],
            tile_send_back.at[at],
            tile_recv_back.at[at],
            (views[0], tile),
        )
        for at, tile in enumerate(tiles[1:])
    ]
    total = dense_ref[pl.ds(tiles[0], 1)][0]
    for at, copy in enumerate(over_tiles):
        copy.wait()
        total = total + landing_ref[at]
    summed_ref[...] = total
    over_views = [
        send(
            summed_ref.at[view],
            out_ref.at[views[0]],
            view_send_back.at[at],
            view_recv_back.at[at],
            (view, tiles[0]),
        )
        for at, view in enumerate(views[1:])
    ]
    out_ref[pl.ds(views[0], 1)] = summed_ref[pl.ds(views[0], 1)]
    for copy in over_views:
        copy.wait()


def update_kernel(
    width,
    height,
    cameras_ref,
    rates_ref,
    grads_ref,
    params_ref,
    first_ref,
    second_ref,
    new_params_ref,
    new_first_ref,
    new_second_ref,
):
    camera = camera_columns(cameras_ref)
    values = [params_ref[at : at + 1, :] for at in range(59)]
    _, pullback = jax.vjp(
        lambda rows: project(rows, camera, float(width), 0.5 * width, 0.5 * height), values
    )
    given = [grads_ref[:, row_at, :] for row_at in range(9)]
    grads = list(pullback(tuple(given[:5] + given[6:]))[0])
    grads[10] = jnp.sum(given[5], axis=0, keepdims=True) * (1.0 - sigmoid(values[10]))
    for at in range(59):
        new_first_ref[at : at + 1, :] = grads[at]
    gradient = new_first_ref[...]
    new_first = beta_one * first_ref[...] + (1.0 - beta_one) * gradient
    new_second = beta_two * second_ref[...] + (1.0 - beta_two) * gradient * gradient
    new_first_ref[...] = new_first
    new_second_ref[...] = new_second
    step_size = rates_ref[...] * (new_first / (1.0 - beta_one**ADAM_STEP))
    new_params_ref[...] = params_ref[...] - step_size / (
        jnp.sqrt(new_second / (1.0 - beta_two**ADAM_STEP)) + adam_eps
    )


def in_vmem(count):
    return [pl.BlockSpec(memory_space=pltpu.VMEM)] * count


def per_device(params, first_moment, second_moment, cameras, target, lists, lengths):
    f32, bf16 = jnp.float32, jnp.bfloat16
    view_count = lax.axis_size("views")
    tile_groups = lax.axis_size("tiles")
    peers = view_count * tile_groups
    owned = params.shape[1]
    tile_dev = target.shape[1]
    list_size = lists.shape[2]
    pixels = target.shape[3]
    width = TILE_COLS * TILE_SIDE
    height = tile_dev * tile_groups // TILE_COLS * TILE_SIDE
    limit = 56 * 1024 * 1024

    dma = pltpu.SemaphoreType.DMA
    semaphores = [
        dma((view_count,)),
        dma((view_count,)),
        dma((tile_groups,)),
        dma((tile_groups,)),
    ]
    by_owner = (tile_groups, view_count, 9, owned)
    block_rows = (view_count, 9, owned)
    blocks = peers * owned // 256
    group = 16
    pair = 2
    row_grads = pl.pallas_call(
        lambda *refs: step_kernel(width, height, *refs),
        out_shape=jax.ShapeDtypeStruct(block_rows, f32),
        in_specs=[pl.BlockSpec(memory_space=pltpu.SMEM)]
        + [pl.BlockSpec(memory_space=pltpu.HBM)] * 4,
        out_specs=pl.BlockSpec(memory_space=pltpu.VMEM),
        scratch_shapes=[
            pltpu.VMEM(cameras.shape, f32),
            pltpu.VMEM(params.shape, f32),
            pltpu.VMEM(lists.shape[1:], jnp.int32),
            pltpu.VMEM((3, tile_dev, pixels), f32),
            dma((4,)),
            pltpu.VMEM(block_rows, f32),
            pltpu.VMEM(by_owner, f32),
            pltpu.VMEM(by_owner, f32),
            pltpu.VMEM((tile_groups - 1,) + block_rows, f32),
            pltpu.VMEM(block_rows, f32),
        ]
        + semaphores
        + semaphores
        + [
            pltpu.VMEM((9, tile_dev, list_size), f32),
            pltpu.VMEM((pair, pixels, 2 * list_size), bf16),
            pltpu.VMEM((pair, pixels, 2 * list_size), bf16),
            pltpu.VMEM((2 * list_size, list_size), bf16),
            pltpu.VMEM((2 * list_size, list_size), bf16),
            pltpu.VMEM((pair, pixels, list_size), f32),
            pltpu.VMEM((pair, pixels, list_size), f32),
            pltpu.VMEM((pair, pixels, list_size), f32),
            pltpu.VMEM((pair, pixels, list_size), f32),
            pltpu.VMEM((pair, pixels, 3 * list_size + 128), bf16),
            pltpu.VMEM((pair, 128, 3 * list_size + 128), bf16),
            pltpu.VMEM((pair, 128, list_size), bf16),
            pltpu.VMEM((group * 32, pair * list_size), bf16),
            pltpu.VMEM((256, pair * list_size), bf16),
            pltpu.VMEM((blocks // group, group * 32, 256), f32),
        ],
        compiler_params=pltpu.CompilerParams(
            collective_id=0, has_side_effects=True, vmem_limit_bytes=limit
        ),
        name="splat_gradients",
    )(lengths[0], cameras, params, lists[0], target[0].transpose(1, 0, 2))

    like = jax.ShapeDtypeStruct(params.shape, f32)
    return pl.pallas_call(
        lambda *refs: update_kernel(width, height, *refs),
        out_shape=(like, like, like),
        in_specs=in_vmem(6),
        out_specs=tuple(in_vmem(3)),
        compiler_params=pltpu.CompilerParams(vmem_limit_bytes=limit),
        name="update_gaussians",
    )(cameras, jnp.asarray(learning), row_grads, params, first_moment, second_moment)


def solution(mesh):
    placed = (
        P(None, ("views", "tiles")),
        P(None, ("views", "tiles")),
        P(None, ("views", "tiles")),
        P(),
        P("views", "tiles", None, None),
        P("views", "tiles", None),
        P("views", "tiles"),
    )
    return jax.shard_map(
        per_device,
        mesh=mesh,
        in_specs=placed,
        out_specs=(
            P(None, ("views", "tiles")),
            P(None, ("views", "tiles")),
            P(None, ("views", "tiles")),
        ),
        check_vma=False,
    )
```

```python
import jax
import jax.numpy as jnp
import numpy as np
from jax import lax
from jax.experimental import pallas as pl
from jax.experimental.pallas import tpu as pltpu
from jax.sharding import PartitionSpec as P

TILE_SIDE = 16
TILE_COLS = 32
ADAM_STEP = 1000


sh_zero = 0.28209479177387814
sh_first = 0.4886025119029199
sh_second = (
    1.0925484305920792,
    -1.0925484305920792,
    0.31539156525252005,
    -1.0925484305920792,
    0.5462742152960396,
)
sh_third = (
    -0.5900435899266435,
    2.890611442640554,
    -0.4570457994644658,
    0.3731763325901154,
    -0.4570457994644658,
    1.445305721320277,
    -0.5900435899266435,
)
beta_one = 0.9
beta_two = 0.999
adam_eps = 1e-15
learning = np.concatenate(
    [
        np.full(3, 0.00016),
        np.full(3, 0.005),
        np.full(4, 0.001),
        np.full(1, 0.05),
        np.full(3, 0.0025),
        np.full(45, 0.000125),
    ]
).astype(np.float32)[:, None]


def matmul_three(left, right):
    return [
        [
            left[row_at][0] * right[0][col_at]
            + left[row_at][1] * right[1][col_at]
            + left[row_at][2] * right[2][col_at]
            for col_at in range(3)
        ]
        for row_at in range(3)
    ]


def camera_rotation(camera):
    cos_a, sin_a = (jnp.cos(camera[0]), jnp.sin(camera[0]))
    cos_b, sin_b = (jnp.cos(camera[1]), jnp.sin(camera[1]))
    cos_c, sin_c = (jnp.cos(camera[2]), jnp.sin(camera[2]))
    around_x = [[1.0, 0.0, 0.0], [0.0, cos_a, -sin_a], [0.0, sin_a, cos_a]]
    around_y = [[cos_b, 0.0, sin_b], [0.0, 1.0, 0.0], [-sin_b, 0.0, cos_b]]
    around_z = [[cos_c, -sin_c, 0.0], [sin_c, cos_c, 0.0], [0.0, 0.0, 1.0]]
    return matmul_three(around_z, matmul_three(around_y, around_x))


def sh_basis(along_x, along_y, along_z):
    square_x, square_y, square_z = (along_x * along_x, along_y * along_y, along_z * along_z)
    both_xy, both_yz, both_xz = (along_x * along_y, along_y * along_z, along_x * along_z)
    return [
        sh_zero + 0.0 * along_x,
        -sh_first * along_y,
        sh_first * along_z,
        -sh_first * along_x,
        sh_second[0] * both_xy,
        sh_second[1] * both_yz,
        sh_second[2] * (2.0 * square_z - square_x - square_y),
        sh_second[3] * both_xz,
        sh_second[4] * (square_x - square_y),
        sh_third[0] * along_y * (3.0 * square_x - square_y),
        sh_third[1] * both_xy * along_z,
        sh_third[2] * along_y * (4.0 * square_z - square_x - square_y),
        sh_third[3] * along_z * (2.0 * square_z - 3.0 * square_x - 3.0 * square_y),
        sh_third[4] * along_x * (4.0 * square_z - square_x - square_y),
        sh_third[5] * along_z * (square_x - square_y),
        sh_third[6] * along_x * (square_x - 3.0 * square_y),
    ]


def project(rows, camera, focal_len, center_x, center_y):
    rotation = camera_rotation(camera)
    means = rows[0:3]
    point = [
        rotation[axis_at][0] * means[0]
        + rotation[axis_at][1] * means[1]
        + rotation[axis_at][2] * means[2]
        + camera[3 + axis_at]
        for axis_at in range(3)
    ]
    inverse_z = 1.0 / point[2]
    screen_u = focal_len * point[0] * inverse_z + center_x
    screen_v = focal_len * point[1] * inverse_z + center_y
    scales = [jnp.exp(value) for value in rows[3:6]]
    norm = rows[6] * rows[6] + rows[7] * rows[7] + rows[8] * rows[8] + rows[9] * rows[9]
    inverse_norm = lax.rsqrt(norm)
    real_part, imag_x, imag_y, imag_z = [value * inverse_norm for value in rows[6:10]]
    spin = [
        [
            1.0 - 2.0 * (imag_y * imag_y + imag_z * imag_z),
            2.0 * (imag_x * imag_y - real_part * imag_z),
            2.0 * (imag_x * imag_z + real_part * imag_y),
        ],
        [
            2.0 * (imag_x * imag_y + real_part * imag_z),
            1.0 - 2.0 * (imag_x * imag_x + imag_z * imag_z),
            2.0 * (imag_y * imag_z - real_part * imag_x),
        ],
        [
            2.0 * (imag_x * imag_z - real_part * imag_y),
            2.0 * (imag_y * imag_z + real_part * imag_x),
            1.0 - 2.0 * (imag_x * imag_x + imag_y * imag_y),
        ],
    ]
    turned = matmul_three(rotation, spin)
    shaped = [
        [turned[row_at][col_at] * scales[col_at] for col_at in range(3)] for row_at in range(3)
    ]
    near_x = [
        focal_len * inverse_z * shaped[0][col_at]
        - focal_len * point[0] * inverse_z * inverse_z * shaped[2][col_at]
        for col_at in range(3)
    ]
    near_y = [
        focal_len * inverse_z * shaped[1][col_at]
        - focal_len * point[1] * inverse_z * inverse_z * shaped[2][col_at]
        for col_at in range(3)
    ]
    cov_a = near_x[0] * near_x[0] + near_x[1] * near_x[1] + near_x[2] * near_x[2] + 0.3
    cov_b = near_x[0] * near_y[0] + near_x[1] * near_y[1] + near_x[2] * near_y[2]
    cov_c = near_y[0] * near_y[0] + near_y[1] * near_y[1] + near_y[2] * near_y[2] + 0.3
    determinant = cov_a * cov_c - cov_b * cov_b
    offset = [
        means[axis_at]
        + rotation[0][axis_at] * camera[3]
        + rotation[1][axis_at] * camera[4]
        + rotation[2][axis_at] * camera[5]
        for axis_at in range(3)
    ]
    inverse_len = lax.rsqrt(offset[0] * offset[0] + offset[1] * offset[1] + offset[2] * offset[2])
    basis = sh_basis(offset[0] * inverse_len, offset[1] * inverse_len, offset[2] * inverse_len)
    colors = [
        0.5 + sum((basis[coef_at] * rows[11 + 3 * coef_at + channel] for coef_at in range(16)))
        for channel in range(3)
    ]
    return (
        screen_u,
        screen_v,
        cov_c / determinant,
        -cov_b / determinant,
        cov_a / determinant,
        colors[0],
        colors[1],
        colors[2],
    )


def rotated(start, count):
    return [lax.rem(start + step, count) for step in range(count)]


def greet(others):
    barrier = pltpu.get_barrier_semaphore()
    for device in others:
        pl.semaphore_signal(
            barrier, inc=1, device_id=device, device_id_type=pl.DeviceIdType.MESH
        )
    return lambda: pl.semaphore_wait(barrier, len(others))


def send(source, landing, send_sem, recv_sem, device):
    copy = pltpu.make_async_remote_copy(
        src_ref=source,
        dst_ref=landing,
        send_sem=send_sem,
        recv_sem=recv_sem,
        device_id=device,
        device_id_type=pl.DeviceIdType.MESH,
    )
    copy.start()
    return copy


def camera_columns(cameras_ref):
    return [cameras_ref[:, at : at + 1] for at in range(6)]


def sigmoid(value):
    return 1.0 / (1.0 + jnp.exp(-value))


def fold(value):
    return value[0:8] + value[8:16]


def wide(row):
    eight = jnp.broadcast_to(row, (8, row.shape[1]))
    return jnp.concatenate([eight, eight], axis=0)


def step_kernel(
    width,
    height,
    lengths_ref,
    cameras_far,
    params_far,
    lists_far,
    target_far,
    out_ref,
    cameras_ref,
    params_ref,
    lists_ref,
    target_ref,
    fetch_sem,
    rows_ref,
    table_ref,
    dense_ref,
    landing_ref,
    rows_send,
    rows_recv,
    grads_send,
    grads_recv,
    picked,
    keeps,
    suffix,
    before,
    after,
    alpha_s,
    ratio_s,
    flow_s,
    weight_s,
    painted,
    paints,
    tints,
    chosen,
    one_hot,
    spread,
):
    f32, bf16 = jnp.float32, jnp.bfloat16
    tile_dev, list_size = lists_ref.shape
    tile_groups, view_count, _, owned = table_ref.shape
    per_owner = owned // 128
    halves = list_size // 128
    views = rotated(lax.axis_index("views"), view_count)
    tiles = rotated(lax.axis_index("tiles"), tile_groups)
    pairs = ((params_far, params_ref), (cameras_far, cameras_ref))
    pairs = pairs + ((lists_far, lists_ref), (target_far, target_ref))
    fetches = [
        pltpu.make_async_copy(far, near, fetch_sem.at[at]) for at, (far, near) in enumerate(pairs)
    ]
    for fetch in fetches:
        fetch.start()
    steps = [(turn, step) for step in range(tile_groups) for turn in range(view_count)][1:]
    everyone_here = greet([(views[turn], tiles[step]) for turn, step in steps])
    for fetch in fetches[:2]:
        fetch.wait()
    values = [params_ref[at : at + 1, :] for at in range(59)]
    made = project(
        values, camera_columns(cameras_ref), float(width), 0.5 * width, 0.5 * height
    )
    opacities = jnp.broadcast_to(sigmoid(values[10]), (view_count, owned))
    for row_at, value in enumerate(made[:5] + (opacities,) + made[5:]):
        rows_ref[:, row_at, :] = value
    everyone_here()
    sent_rows = [
        send(
            rows_ref.at[views[turn]],
            table_ref.at[tiles[0], views[0]],
            rows_send.at[turn, step],
            rows_recv.at[turn, step],
            (views[turn], tiles[step]),
        )
        for turn, step in steps
    ]
    table_ref[pl.ds(tiles[0], 1), pl.ds(views[0], 1)] = rows_ref[pl.ds(views[0], 1)][None]

    row_ids = lax.broadcasted_iota(jnp.int32, (list_size, list_size), 0)
    col_ids = lax.broadcasted_iota(jnp.int32, (list_size, list_size), 1)
    for piece in range(2):
        here = slice(piece * list_size, (piece + 1) * list_size)
        before[here, :] = (row_ids < col_ids).astype(f32).astype(bf16)
    after[...] = (row_ids > col_ids).astype(f32).astype(bf16)
    spread[...] = jnp.zeros_like(spread)
    tints[...] = jnp.zeros_like(tints)
    paints[...] = jnp.zeros_like(paints)
    painted[:, :, 3 * list_size :] = jnp.zeros(
        (painted.shape[0], painted.shape[1], 128), bf16
    )
    channels = lax.broadcasted_iota(jnp.int32, (16, 128), 0)
    pieces_at = lax.broadcasted_iota(jnp.int32, (16, 128), 1)
    same = (channels % 3 == pieces_at % 3) & (channels < 9) & (pieces_at < 9)
    for slot in range(paints.shape[0]):
        paints[slot, 0:16, 3 * list_size :] = jnp.where(same, -1.0, 0.0).astype(bf16)
    lane_ids = lax.broadcasted_iota(jnp.int32, (1, list_size), 1)
    pixel_ids = lax.broadcasted_iota(jnp.int32, (16, list_size), 0).astype(f32)
    column_ids = lax.broadcasted_iota(jnp.int32, (256, list_size), 0)
    first_tile = tiles[0] * tile_dev
    for fetch in fetches[2:]:
        fetch.wait()
    entries = lists_ref[...]
    block_of = entries >> 7
    column_of = entries & 127

    def gather_from(tile_group, carry):
        carry = list(carry)
        for view in range(view_count):
            for part in range(per_owner):
                lanes = slice(part * 128, part * 128 + 128)
                block = (view * tile_groups + tile_group) * per_owner + part
                for half in range(halves):
                    here = slice(half * 128, half * 128 + 128)
                    mask = block_of[:, here] == block
                    column = column_of[:, here]
                    for row_at in range(9):
                        line = table_ref[tile_group, view, row_at : row_at + 1, lanes]
                        got = jnp.take_along_axis(
                            jnp.broadcast_to(line, (tile_dev, 128)),
                            column,
                            axis=1,
                            mode="promise_in_bounds",
                        )
                        slot = half * 9 + row_at
                        carry[slot] = jnp.where(mask, got, carry[slot])
        return tuple(carry)

    def wait_rows(turn, step, source):
        sender = (views[(view_count - turn) % view_count], source)
        pltpu.make_async_remote_copy(
            src_ref=rows_ref.at[sender[0]],
            dst_ref=table_ref.at[source, sender[0]],
            send_sem=rows_send.at[turn, step],
            recv_sem=rows_recv.at[turn, step],
            device_id=sender,
            device_id_type=pl.DeviceIdType.MESH,
        ).wait_recv()

    def gather_arrived(step, carry):
        source = lax.rem(tiles[0] + tile_groups - step, tile_groups)
        for turn in range(view_count):
            wait_rows(turn, step, source)
        return gather_from(source, carry)

    for turn in range(1, view_count):
        wait_rows(turn, 0, tiles[0])
    gathered = tuple(jnp.zeros((tile_dev, 128), f32) for _ in range(halves * 9))
    gathered = gather_from(tiles[0], gathered)
    gathered = lax.fori_loop(1, tile_groups, gather_arrived, gathered)
    for half in range(halves):
        for row_at in range(9):
            picked[row_at, :, half * 128 : half * 128 + 128] = gathered[half * 9 + row_at]
    for copy in sent_rows:
        copy.wait_send()
    group = spread.shape[1] // 32
    pair = keeps.shape[0]
    lines = [slice(line * 16, line * 16 + 16) for line in range(TILE_SIDE)]

    def load_tile(tile_at):
        tile_id = first_tile + tile_at
        left = (tile_id % TILE_COLS * TILE_SIDE).astype(f32) + 0.5
        top = (tile_id // TILE_COLS * TILE_SIDE).astype(f32) + 0.5
        rows = [picked[row_at, pl.ds(tile_at, 1), :] for row_at in range(9)]
        rows[5] = jnp.where(lane_ids < lengths_ref[tile_at], rows[5], 0.0)
        delta_x = (pixel_ids + left) - wide(rows[0])
        return rows, delta_x, top

    def delta_y_at(rows, top, line):
        return (top + float(line)) - wide(rows[1])

    def alphas_of(slot, rows, delta_x, top):
        opacity = wide(rows[5])
        part_a = wide(-0.5 * rows[2]) * delta_x * delta_x
        part_b = wide(-rows[3]) * delta_x
        half_c = wide(-0.5 * rows[4])
        for line, here in enumerate(lines):
            delta_y = delta_y_at(rows, top, line)
            alphas = opacity * jnp.exp(part_a + delta_y * (part_b + half_c * delta_y))
            log_keep = jnp.log(1.0 - alphas)
            high = log_keep.astype(bf16)
            keeps[slot, here, 0:list_size] = high
            keeps[slot, here, list_size : 2 * list_size] = (log_keep - high.astype(f32)).astype(bf16)
            alpha_s[slot, here, :] = alphas
            ratio_s[slot, here, :] = alphas * jnp.exp(-log_keep)

    def split(value):
        high = value.astype(bf16)
        return high, (value - high.astype(f32)).astype(bf16)

    def colors_of(slot, tile_at, rows):
        empty = jnp.zeros((7, list_size), f32)
        colors = jnp.concatenate(rows[6:9], axis=0)
        high = colors.astype(bf16).astype(f32)
        middle = (colors - high).astype(bf16).astype(f32)
        low = colors - high - middle
        highs = jnp.concatenate([high, high, high, empty], axis=0).astype(bf16)
        lows = jnp.concatenate([middle, middle, middle, empty], axis=0).astype(bf16)
        paints[slot, 0:16, 0:list_size] = highs
        paints[slot, 0:16, list_size : 2 * list_size] = highs
        paints[slot, 0:16, 2 * list_size : 3 * list_size] = lows
        tints[slot, 0:16, :] = jnp.concatenate([high, middle, low, empty], axis=0).astype(bf16)
        wanted = jnp.concatenate(
            [target_ref[channel, pl.ds(tile_at, 1), :] for channel in range(3)], axis=0
        )
        high = wanted.astype(bf16).astype(f32)
        middle = (wanted - high).astype(bf16).astype(f32)
        low = wanted - high - middle
        wanted = jnp.concatenate([high, middle, low, jnp.zeros((7, wanted.shape[1]), f32)], axis=0)
        painted[slot, :, 3 * list_size : 3 * list_size + 16] = wanted.T.astype(bf16)

    def weights_of(slot, passed):
        for here in lines:
            weight = jnp.exp(passed[here]) * alpha_s[slot, here, :]
            high, low = split(weight)
            weight_s[slot, here, :] = weight
            painted[slot, here, 0:list_size] = high
            painted[slot, here, list_size : 2 * list_size] = low
            painted[slot, here, 2 * list_size : 3 * list_size] = high

    def signs_of(gaps):
        return jnp.where(gaps > 0.0, 1.0, jnp.where(gaps < 0.0, -1.0, 0.0))

    def color_grads(slot, signs):
        turned = signs.T[0:16].astype(bf16)
        both = jnp.dot(turned, painted[slot, :, 0 : 2 * list_size], preferred_element_type=f32)
        return both[0:3, 0:list_size] + both[0:3, list_size : 2 * list_size]

    def flows_of(slot, tinted):
        for here in lines:
            flow = weight_s[slot, here, :] * tinted[here]
            suffix[slot, here, :] = flow.astype(bf16)
            flow_s[slot, here, :] = flow

    def grads_of(slot, rows, delta_x, top, behind, color_sums):
        sums = [jnp.zeros((8, list_size), f32) for _ in range(6)]
        for line, here in enumerate(lines):
            delta_y = delta_y_at(rows, top, line)[0:8]
            pull = flow_s[slot, here, :] - behind[here] * ratio_s[slot, here, :]
            pull_x = pull * delta_x
            pull_xx = fold(pull_x * delta_x)
            pull_x = fold(pull_x)
            pull = fold(pull)
            pull_y = pull * delta_y
            terms = (pull, pull_x, pull_y, pull_xx, pull_x * delta_y, pull_y * delta_y)
            sums = [total + term for total, term in zip(sums, terms)]
        flat, by_x, by_y, by_xx, by_xy, by_yy = [
            jnp.sum(total, axis=0, keepdims=True) for total in sums
        ]
        _, _, con_a, con_b, con_c = rows[:5]
        return jnp.concatenate(
            [
                con_a * by_x + con_b * by_y,
                con_b * by_x + con_c * by_y,
                -0.5 * by_xx,
                -by_xy,
                -0.5 * by_yy,
                flat,
            ]
            + [color_sums]
            + [jnp.zeros((7, list_size), f32)],
            axis=0,
        )

    def some_tiles(step, carry):
        slots = range(pair)
        at = [step * pair + slot for slot in slots]
        arrived = [load_tile(tile_at) for tile_at in at]
        passed, gaps, tinted, color_sums, behind = [], [], [], [], []
        for slot in slots:
            alphas_of(slot, *arrived[slot])
            passed.append(jnp.dot(keeps[slot], before[...], preferred_element_type=f32))
            colors_of(slot, at[slot], arrived[slot][0])
        for slot in slots:
            weights_of(slot, passed[slot])
            gaps.append(
                lax.dot_general(
                    painted[slot], paints[slot], (((1,), (1,)), ((), ())), preferred_element_type=f32
                )
            )
        for slot in slots:
            signs = signs_of(gaps[slot])
            tinted.append(jnp.dot(signs.astype(bf16), tints[slot], preferred_element_type=f32))
            color_sums.append(color_grads(slot, signs))
        for slot in slots:
            flows_of(slot, tinted[slot])
            behind.append(jnp.dot(suffix[slot], after[...], preferred_element_type=f32))
        owners, pieces = [], []
        for slot in slots:
            grads = grads_of(slot, *arrived[slot], behind[slot], color_sums[slot])
            high = grads.astype(bf16).astype(f32)
            pieces.append(jnp.concatenate([high, grads - high], axis=0))
            ids = lists_ref[pl.ds(at[slot], 1), :]
            owners.append(wide(ids >> 8))
            lanes = slice(slot * list_size, (slot + 1) * list_size)
            one_hot[:, lanes] = (column_ids == (ids & 255)).astype(f32).astype(bf16)

        def spread_group(group_at, carry):
            for slot in slots:
                lanes = slice(slot * list_size, (slot + 1) * list_size)
                for block in range(group):
                    mask = owners[slot] == group_at * group + block
                    mask = jnp.concatenate([mask, mask], axis=0)
                    chosen[block * 32 : block * 32 + 32, lanes] = jnp.where(
                        mask, pieces[slot], 0.0
                    ).astype(bf16)
            spread[group_at] += lax.dot_general(
                chosen[...], one_hot[...], (((1,), (1,)), ((), ())), preferred_element_type=f32
            )
            return carry

        if spread.shape[0] == 1:
            spread_group(0, 0)
        else:
            lax.fori_loop(0, spread.shape[0], spread_group, 0)
        return carry

    lax.fori_loop(0, tile_dev // pair, some_tiles, 0)

    def finish_group(group_at, carry):
        for block in range(group):
            both = spread[group_at, block * 32 : block * 32 + 32, :]
            total = both[0:16] + both[16:32]
            for half in range(2):
                chunk = block * 2 + half
                owner = group_at * (2 * group // per_owner) + chunk // per_owner
                lanes = chunk % per_owner * 128
                dense_ref[owner % tile_groups, owner // tile_groups, :, lanes : lanes + 128] = total[
                    0:9, half * 128 : half * 128 + 128
                ]
        return carry

    if spread.shape[0] == 1:
        finish_group(0, 0)
    else:
        lax.fori_loop(0, spread.shape[0], finish_group, 0)

    sent_grads = [
        send(
            dense_ref.at[tiles[step], views[turn]],
            landing_ref.at[turn, step],
            grads_send.at[turn, step],
            grads_recv.at[turn, step],
            (views[turn], tiles[step]),
        )
        for turn, step in steps
    ]
    totals = [None] * view_count
    totals[0] = dense_ref[pl.ds(tiles[0], 1), pl.ds(views[0], 1)][0, 0]
    for copy, (turn, step) in zip(sent_grads, steps):
        copy.wait()
        block = landing_ref[turn, step]
        totals[turn] = block if totals[turn] is None else totals[turn] + block
    for turn in range(view_count):
        sender = views[(view_count - turn) % view_count]
        out_ref[pl.ds(sender, 1)] = totals[turn][None]


def update_kernel(
    width,
    height,
    cameras_ref,
    rates_ref,
    grads_ref,
    params_ref,
    first_ref,
    second_ref,
    new_params_ref,
    new_first_ref,
    new_second_ref,
):
    camera = camera_columns(cameras_ref)
    values = [params_ref[at : at + 1, :] for at in range(59)]
    _, pullback = jax.vjp(
        lambda rows: project(rows, camera, float(width), 0.5 * width, 0.5 * height), values
    )
    given = [grads_ref[:, row_at, :] for row_at in range(9)]
    grads = list(pullback(tuple(given[:5] + given[6:]))[0])
    grads[10] = jnp.sum(given[5], axis=0, keepdims=True) * (1.0 - sigmoid(values[10]))
    for at in range(59):
        new_first_ref[at : at + 1, :] = grads[at]
    gradient = new_first_ref[...]
    new_first = beta_one * first_ref[...] + (1.0 - beta_one) * gradient
    new_second = beta_two * second_ref[...] + (1.0 - beta_two) * gradient * gradient
    new_first_ref[...] = new_first
    new_second_ref[...] = new_second
    step_size = rates_ref[...] * (new_first / (1.0 - beta_one**ADAM_STEP))
    new_params_ref[...] = params_ref[...] - step_size / (
        jnp.sqrt(new_second / (1.0 - beta_two**ADAM_STEP)) + adam_eps
    )


def in_vmem(count):
    return [pl.BlockSpec(memory_space=pltpu.VMEM)] * count


def per_device(params, first_moment, second_moment, cameras, target, lists, lengths):
    f32, bf16 = jnp.float32, jnp.bfloat16
    view_count = lax.axis_size("views")
    tile_groups = lax.axis_size("tiles")
    peers = view_count * tile_groups
    owned = params.shape[1]
    tile_dev = target.shape[1]
    list_size = lists.shape[2]
    pixels = target.shape[3]
    width = TILE_COLS * TILE_SIDE
    height = tile_dev * tile_groups // TILE_COLS * TILE_SIDE
    limit = 56 * 1024 * 1024

    dma = pltpu.SemaphoreType.DMA
    semaphores = [dma((view_count, tile_groups))] * 4
    by_owner = (tile_groups, view_count, 9, owned)
    block_rows = (view_count, 9, owned)
    blocks = peers * owned // 256
    group = 16
    pair = 2
    row_grads = pl.pallas_call(
        lambda *refs: step_kernel(width, height, *refs),
        out_shape=jax.ShapeDtypeStruct(block_rows, f32),
        in_specs=[pl.BlockSpec(memory_space=pltpu.SMEM)]
        + [pl.BlockSpec(memory_space=pltpu.HBM)] * 4,
        out_specs=pl.BlockSpec(memory_space=pltpu.VMEM),
        scratch_shapes=[
            pltpu.VMEM(cameras.shape, f32),
            pltpu.VMEM(params.shape, f32),
            pltpu.VMEM(lists.shape[1:], jnp.int32),
            pltpu.VMEM((3, tile_dev, pixels), f32),
            dma((4,)),
            pltpu.VMEM(block_rows, f32),
            pltpu.VMEM(by_owner, f32),
            pltpu.VMEM(by_owner, f32),
            pltpu.VMEM((view_count, tile_groups, 9, owned), f32),
        ]
        + semaphores
        + [
            pltpu.VMEM((9, tile_dev, list_size), f32),
            pltpu.VMEM((pair, pixels, 2 * list_size), bf16),
            pltpu.VMEM((pair, pixels, list_size), bf16),
            pltpu.VMEM((2 * list_size, list_size), bf16),
            pltpu.VMEM((list_size, list_size), bf16),
            pltpu.VMEM((pair, pixels, list_size), f32),
            pltpu.VMEM((pair, pixels, list_size), f32),
            pltpu.VMEM((pair, pixels, list_size), f32),
            pltpu.VMEM((pair, pixels, list_size), f32),
            pltpu.VMEM((pair, pixels, 3 * list_size + 128), bf16),
            pltpu.VMEM((pair, 128, 3 * list_size + 128), bf16),
            pltpu.VMEM((pair, 128, list_size), bf16),
            pltpu.VMEM((group * 32, pair * list_size), bf16),
            pltpu.VMEM((256, pair * list_size), bf16),
            pltpu.VMEM((blocks // group, group * 32, 256), f32),
        ],
        compiler_params=pltpu.CompilerParams(
            collective_id=0, has_side_effects=True, vmem_limit_bytes=limit
        ),
        name="splat_gradients",
    )(lengths[0], cameras, params, lists[0], target[0].transpose(1, 0, 2))

    like = jax.ShapeDtypeStruct(params.shape, f32)
    return pl.pallas_call(
        lambda *refs: update_kernel(width, height, *refs),
        out_shape=(like, like, like),
        in_specs=in_vmem(6),
        out_specs=tuple(in_vmem(3)),
        compiler_params=pltpu.CompilerParams(vmem_limit_bytes=limit),
        name="update_gaussians",
    )(cameras, jnp.asarray(learning), row_grads, params, first_moment, second_moment)


def solution(mesh):
    placed = (
        P(None, ("views", "tiles")),
        P(None, ("views", "tiles")),
        P(None, ("views", "tiles")),
        P(),
        P("views", "tiles", None, None),
        P("views", "tiles", None),
        P("views", "tiles"),
    )
    return jax.shard_map(
        per_device,
        mesh=mesh,
        in_specs=placed,
        out_specs=(
            P(None, ("views", "tiles")),
            P(None, ("views", "tiles")),
            P(None, ("views", "tiles")),
        ),
        check_vma=False,
    )
```

```python
import jax
import jax.numpy as jnp
import numpy as np
from jax import lax
from jax.experimental import pallas as pl
from jax.experimental.pallas import tpu as pltpu
from jax.sharding import PartitionSpec as P

TILE_SIDE = 16
TILE_COLS = 32
ADAM_STEP = 1000


sh_zero = 0.28209479177387814
sh_first = 0.4886025119029199
sh_second = (
    1.0925484305920792,
    -1.0925484305920792,
    0.31539156525252005,
    -1.0925484305920792,
    0.5462742152960396,
)
sh_third = (
    -0.5900435899266435,
    2.890611442640554,
    -0.4570457994644658,
    0.3731763325901154,
    -0.4570457994644658,
    1.445305721320277,
    -0.5900435899266435,
)
beta_one = 0.9
beta_two = 0.999
adam_eps = 1e-15
learning = np.concatenate(
    [
        np.full(3, 0.00016),
        np.full(3, 0.005),
        np.full(4, 0.001),
        np.full(1, 0.05),
        np.full(3, 0.0025),
        np.full(45, 0.000125),
    ]
).astype(np.float32)[:, None]


def matmul_three(left, right):
    return [
        [
            left[row_at][0] * right[0][col_at]
            + left[row_at][1] * right[1][col_at]
            + left[row_at][2] * right[2][col_at]
            for col_at in range(3)
        ]
        for row_at in range(3)
    ]


def camera_rotation(camera):
    cos_a, sin_a = (jnp.cos(camera[0]), jnp.sin(camera[0]))
    cos_b, sin_b = (jnp.cos(camera[1]), jnp.sin(camera[1]))
    cos_c, sin_c = (jnp.cos(camera[2]), jnp.sin(camera[2]))
    around_x = [[1.0, 0.0, 0.0], [0.0, cos_a, -sin_a], [0.0, sin_a, cos_a]]
    around_y = [[cos_b, 0.0, sin_b], [0.0, 1.0, 0.0], [-sin_b, 0.0, cos_b]]
    around_z = [[cos_c, -sin_c, 0.0], [sin_c, cos_c, 0.0], [0.0, 0.0, 1.0]]
    return matmul_three(around_z, matmul_three(around_y, around_x))


def sh_basis(along_x, along_y, along_z):
    square_x, square_y, square_z = (along_x * along_x, along_y * along_y, along_z * along_z)
    both_xy, both_yz, both_xz = (along_x * along_y, along_y * along_z, along_x * along_z)
    return [
        sh_zero + 0.0 * along_x,
        -sh_first * along_y,
        sh_first * along_z,
        -sh_first * along_x,
        sh_second[0] * both_xy,
        sh_second[1] * both_yz,
        sh_second[2] * (2.0 * square_z - square_x - square_y),
        sh_second[3] * both_xz,
        sh_second[4] * (square_x - square_y),
        sh_third[0] * along_y * (3.0 * square_x - square_y),
        sh_third[1] * both_xy * along_z,
        sh_third[2] * along_y * (4.0 * square_z - square_x - square_y),
        sh_third[3] * along_z * (2.0 * square_z - 3.0 * square_x - 3.0 * square_y),
        sh_third[4] * along_x * (4.0 * square_z - square_x - square_y),
        sh_third[5] * along_z * (square_x - square_y),
        sh_third[6] * along_x * (square_x - 3.0 * square_y),
    ]


def project(rows, camera, focal_len, center_x, center_y):
    rotation = camera_rotation(camera)
    means = rows[0:3]
    point = [
        rotation[axis_at][0] * means[0]
        + rotation[axis_at][1] * means[1]
        + rotation[axis_at][2] * means[2]
        + camera[3 + axis_at]
        for axis_at in range(3)
    ]
    inverse_z = 1.0 / point[2]
    screen_u = focal_len * point[0] * inverse_z + center_x
    screen_v = focal_len * point[1] * inverse_z + center_y
    scales = [jnp.exp(value) for value in rows[3:6]]
    norm = rows[6] * rows[6] + rows[7] * rows[7] + rows[8] * rows[8] + rows[9] * rows[9]
    inverse_norm = lax.rsqrt(norm)
    real_part, imag_x, imag_y, imag_z = [value * inverse_norm for value in rows[6:10]]
    spin = [
        [
            1.0 - 2.0 * (imag_y * imag_y + imag_z * imag_z),
            2.0 * (imag_x * imag_y - real_part * imag_z),
            2.0 * (imag_x * imag_z + real_part * imag_y),
        ],
        [
            2.0 * (imag_x * imag_y + real_part * imag_z),
            1.0 - 2.0 * (imag_x * imag_x + imag_z * imag_z),
            2.0 * (imag_y * imag_z - real_part * imag_x),
        ],
        [
            2.0 * (imag_x * imag_z - real_part * imag_y),
            2.0 * (imag_y * imag_z + real_part * imag_x),
            1.0 - 2.0 * (imag_x * imag_x + imag_y * imag_y),
        ],
    ]
    turned = matmul_three(rotation, spin)
    shaped = [
        [turned[row_at][col_at] * scales[col_at] for col_at in range(3)] for row_at in range(3)
    ]
    near_x = [
        focal_len * inverse_z * shaped[0][col_at]
        - focal_len * point[0] * inverse_z * inverse_z * shaped[2][col_at]
        for col_at in range(3)
    ]
    near_y = [
        focal_len * inverse_z * shaped[1][col_at]
        - focal_len * point[1] * inverse_z * inverse_z * shaped[2][col_at]
        for col_at in range(3)
    ]
    cov_a = near_x[0] * near_x[0] + near_x[1] * near_x[1] + near_x[2] * near_x[2] + 0.3
    cov_b = near_x[0] * near_y[0] + near_x[1] * near_y[1] + near_x[2] * near_y[2]
    cov_c = near_y[0] * near_y[0] + near_y[1] * near_y[1] + near_y[2] * near_y[2] + 0.3
    determinant = cov_a * cov_c - cov_b * cov_b
    offset = [
        means[axis_at]
        + rotation[0][axis_at] * camera[3]
        + rotation[1][axis_at] * camera[4]
        + rotation[2][axis_at] * camera[5]
        for axis_at in range(3)
    ]
    inverse_len = lax.rsqrt(offset[0] * offset[0] + offset[1] * offset[1] + offset[2] * offset[2])
    basis = sh_basis(offset[0] * inverse_len, offset[1] * inverse_len, offset[2] * inverse_len)
    colors = [
        0.5 + sum((basis[coef_at] * rows[11 + 3 * coef_at + channel] for coef_at in range(16)))
        for channel in range(3)
    ]
    return (
        screen_u,
        screen_v,
        cov_c / determinant,
        -cov_b / determinant,
        cov_a / determinant,
        colors[0],
        colors[1],
        colors[2],
    )


def rotated(start, count):
    return [lax.rem(start + step, count) for step in range(count)]


def greet(others):
    barrier = pltpu.get_barrier_semaphore()
    for device in others:
        pl.semaphore_signal(
            barrier, inc=1, device_id=device, device_id_type=pl.DeviceIdType.MESH
        )
    return lambda: pl.semaphore_wait(barrier, len(others))


def send(source, landing, send_sem, recv_sem, device):
    copy = pltpu.make_async_remote_copy(
        src_ref=source,
        dst_ref=landing,
        send_sem=send_sem,
        recv_sem=recv_sem,
        device_id=device,
        device_id_type=pl.DeviceIdType.MESH,
    )
    copy.start()
    return copy


def camera_columns(cameras_ref):
    return [cameras_ref[:, at : at + 1] for at in range(6)]


def sigmoid(value):
    return 1.0 / (1.0 + jnp.exp(-value))


def fold(value):
    return value[0:8] + value[8:16]


def wide(row):
    eight = jnp.broadcast_to(row, (8, row.shape[1]))
    return jnp.concatenate([eight, eight], axis=0)


def step_kernel(
    width,
    height,
    lengths_ref,
    cameras_far,
    params_far,
    lists_far,
    target_far,
    out_ref,
    cameras_ref,
    params_ref,
    lists_ref,
    target_ref,
    fetch_sem,
    rows_ref,
    table_ref,
    dense_ref,
    landing_ref,
    rows_send,
    rows_recv,
    grads_send,
    grads_recv,
    picked,
    keeps,
    suffix,
    before,
    after,
    alpha_s,
    ratio_s,
    flow_s,
    weight_s,
    painted,
    paints,
    tints,
    chosen,
    one_hot,
    spread,
):
    f32, bf16 = jnp.float32, jnp.bfloat16
    tile_dev, list_size = lists_ref.shape
    tile_groups, view_count, _, owned = table_ref.shape
    per_owner = owned // 128
    halves = list_size // 128
    views = rotated(lax.axis_index("views"), view_count)
    tiles = rotated(lax.axis_index("tiles"), tile_groups)
    pairs = ((params_far, params_ref), (cameras_far, cameras_ref))
    pairs = pairs + ((lists_far, lists_ref), (target_far, target_ref))
    fetches = [
        pltpu.make_async_copy(far, near, fetch_sem.at[at]) for at, (far, near) in enumerate(pairs)
    ]
    for fetch in fetches:
        fetch.start()
    steps = [(turn, step) for step in range(tile_groups) for turn in range(view_count)][1:]
    everyone_here = greet([(views[turn], tiles[step]) for turn, step in steps])
    for fetch in fetches[:2]:
        fetch.wait()
    values = [params_ref[at : at + 1, :] for at in range(59)]
    made = project(
        values, camera_columns(cameras_ref), float(width), 0.5 * width, 0.5 * height
    )
    opacities = jnp.broadcast_to(sigmoid(values[10]), (view_count, owned))
    for row_at, value in enumerate(made[:5] + (opacities,) + made[5:]):
        rows_ref[:, row_at, :] = value
    everyone_here()
    sent_rows = [
        send(
            rows_ref.at[views[turn]],
            table_ref.at[tiles[0], views[0]],
            rows_send.at[turn, step],
            rows_recv.at[turn, step],
            (views[turn], tiles[step]),
        )
        for turn, step in steps
    ]
    table_ref[pl.ds(tiles[0], 1), pl.ds(views[0], 1)] = rows_ref[pl.ds(views[0], 1)][None]

    row_ids = lax.broadcasted_iota(jnp.int32, (list_size, list_size), 0)
    col_ids = lax.broadcasted_iota(jnp.int32, (list_size, list_size), 1)
    for piece in range(2):
        here = slice(piece * list_size, (piece + 1) * list_size)
        before[here, :] = (row_ids < col_ids).astype(f32).astype(bf16)
    after[...] = (row_ids > col_ids).astype(f32).astype(bf16)
    spread[...] = jnp.zeros_like(spread)
    tints[...] = jnp.zeros_like(tints)
    paints[...] = jnp.zeros_like(paints)
    painted[:, :, 2 * list_size :] = jnp.zeros(
        (painted.shape[0], painted.shape[1], 128), bf16
    )
    channels = lax.broadcasted_iota(jnp.int32, (16, 128), 0)
    pieces_at = lax.broadcasted_iota(jnp.int32, (16, 128), 1)
    same = (channels % 3 == pieces_at % 3) & (channels < 9) & (pieces_at < 9)
    for slot in range(paints.shape[0]):
        paints[slot, 0:16, 2 * list_size :] = jnp.where(same, -1.0, 0.0).astype(bf16)
    lane_ids = lax.broadcasted_iota(jnp.int32, (1, list_size), 1)
    pixel_ids = lax.broadcasted_iota(jnp.int32, (16, list_size), 0).astype(f32)
    column_ids = lax.broadcasted_iota(jnp.int32, (256, list_size), 0)
    first_tile = tiles[0] * tile_dev
    for fetch in fetches[2:]:
        fetch.wait()
    entries = lists_ref[...]
    block_of = entries >> 7
    column_of = entries & 127

    def gather_from(tile_group, carry):
        carry = list(carry)
        for view in range(view_count):
            for part in range(per_owner):
                lanes = slice(part * 128, part * 128 + 128)
                block = (view * tile_groups + tile_group) * per_owner + part
                for half in range(halves):
                    here = slice(half * 128, half * 128 + 128)
                    mask = block_of[:, here] == block
                    column = column_of[:, here]
                    for row_at in range(9):
                        line = table_ref[tile_group, view, row_at : row_at + 1, lanes]
                        got = jnp.take_along_axis(
                            jnp.broadcast_to(line, (tile_dev, 128)),
                            column,
                            axis=1,
                            mode="promise_in_bounds",
                        )
                        slot = half * 9 + row_at
                        carry[slot] = jnp.where(mask, got, carry[slot])
        return tuple(carry)

    def wait_rows(turn, step, source):
        sender = (views[(view_count - turn) % view_count], source)
        pltpu.make_async_remote_copy(
            src_ref=rows_ref.at[sender[0]],
            dst_ref=table_ref.at[source, sender[0]],
            send_sem=rows_send.at[turn, step],
            recv_sem=rows_recv.at[turn, step],
            device_id=sender,
            device_id_type=pl.DeviceIdType.MESH,
        ).wait_recv()

    def gather_arrived(step, carry):
        source = lax.rem(tiles[0] + tile_groups - step, tile_groups)
        for turn in range(view_count):
            wait_rows(turn, step, source)
        return gather_from(source, carry)

    for turn in range(1, view_count):
        wait_rows(turn, 0, tiles[0])
    gathered = tuple(jnp.zeros((tile_dev, 128), f32) for _ in range(halves * 9))
    gathered = gather_from(tiles[0], gathered)
    gathered = lax.fori_loop(1, tile_groups, gather_arrived, gathered)
    for half in range(halves):
        for row_at in range(9):
            picked[row_at, :, half * 128 : half * 128 + 128] = gathered[half * 9 + row_at]
    for copy in sent_rows:
        copy.wait_send()
    group = spread.shape[1] // 32
    pair = keeps.shape[0]
    lines = [slice(line * 16, line * 16 + 16) for line in range(TILE_SIDE)]

    def load_tile(tile_at):
        tile_id = first_tile + tile_at
        left = (tile_id % TILE_COLS * TILE_SIDE).astype(f32) + 0.5
        top = (tile_id // TILE_COLS * TILE_SIDE).astype(f32) + 0.5
        rows = [picked[row_at, pl.ds(tile_at, 1), :] for row_at in range(9)]
        rows[5] = jnp.where(lane_ids < lengths_ref[tile_at], rows[5], 0.0)
        delta_x = (pixel_ids + left) - wide(rows[0])
        return rows, delta_x, top

    def delta_y_at(rows, top, line):
        return (top + float(line)) - wide(rows[1])

    def alphas_of(slot, rows, delta_x, top):
        opacity = wide(rows[5])
        part_a = wide(-0.5 * rows[2]) * delta_x * delta_x
        part_b = wide(-rows[3]) * delta_x
        half_c = wide(-0.5 * rows[4])
        for line, here in enumerate(lines):
            delta_y = delta_y_at(rows, top, line)
            alphas = opacity * jnp.exp(part_a + delta_y * (part_b + half_c * delta_y))
            log_keep = jnp.log(1.0 - alphas)
            high = log_keep.astype(bf16)
            keeps[slot, here, 0:list_size] = high
            keeps[slot, here, list_size : 2 * list_size] = (log_keep - high.astype(f32)).astype(bf16)
            alpha_s[slot, here, :] = alphas
            ratio_s[slot, here, :] = alphas * jnp.exp(-log_keep)

    def split(value):
        high = value.astype(bf16)
        return high, (value - high.astype(f32)).astype(bf16)

    def colors_of(slot, tile_at, rows):
        empty = jnp.zeros((7, list_size), f32)
        colors = jnp.concatenate(rows[6:9], axis=0)
        high = colors.astype(bf16).astype(f32)
        middle = (colors - high).astype(bf16).astype(f32)
        low = colors - high - middle
        highs = jnp.concatenate([high, high, high, empty], axis=0).astype(bf16)
        lows = jnp.concatenate([middle, middle, middle, empty], axis=0).astype(bf16)
        paints[slot, 0:16, 0:list_size] = highs
        paints[slot, 0:16, list_size : 2 * list_size] = highs
        paints[slot, 64:80, 0:list_size] = lows
        tints[slot, 0:16, :] = jnp.concatenate([high, middle, low, empty], axis=0).astype(bf16)
        wanted = jnp.concatenate(
            [target_ref[channel, pl.ds(tile_at, 1), :] for channel in range(3)], axis=0
        )
        high = wanted.astype(bf16).astype(f32)
        middle = (wanted - high).astype(bf16).astype(f32)
        low = wanted - high - middle
        wanted = jnp.concatenate([high, middle, low, jnp.zeros((7, wanted.shape[1]), f32)], axis=0)
        painted[slot, :, 2 * list_size : 2 * list_size + 16] = wanted.T.astype(bf16)

    def weights_of(slot, passed):
        for here in lines:
            weight = jnp.exp(passed[here]) * alpha_s[slot, here, :]
            high, low = split(weight)
            weight_s[slot, here, :] = weight
            painted[slot, here, 0:list_size] = high
            painted[slot, here, list_size : 2 * list_size] = low

    def signs_of(gaps):
        return jnp.where(gaps > 0.0, 1.0, jnp.where(gaps < 0.0, -1.0, 0.0))

    def color_grads(slot, signs):
        turned = signs.T[0:16].astype(bf16)
        both = jnp.dot(turned, painted[slot, :, 0 : 2 * list_size], preferred_element_type=f32)
        return both[0:3, 0:list_size] + both[0:3, list_size : 2 * list_size]

    def flows_of(slot, tinted):
        for here in lines:
            flow = weight_s[slot, here, :] * tinted[here]
            suffix[slot, here, :] = flow.astype(bf16)
            flow_s[slot, here, :] = flow

    def grads_of(slot, rows, delta_x, top, behind, color_sums):
        sums = [jnp.zeros((8, list_size), f32) for _ in range(6)]
        for line, here in enumerate(lines):
            delta_y = delta_y_at(rows, top, line)[0:8]
            pull = flow_s[slot, here, :] - behind[here] * ratio_s[slot, here, :]
            pull_x = pull * delta_x
            pull_xx = fold(pull_x * delta_x)
            pull_x = fold(pull_x)
            pull = fold(pull)
            pull_y = pull * delta_y
            terms = (pull, pull_x, pull_y, pull_xx, pull_x * delta_y, pull_y * delta_y)
            sums = [total + term for total, term in zip(sums, terms)]
        flat, by_x, by_y, by_xx, by_xy, by_yy = [
            jnp.sum(total, axis=0, keepdims=True) for total in sums
        ]
        _, _, con_a, con_b, con_c = rows[:5]
        return jnp.concatenate(
            [
                con_a * by_x + con_b * by_y,
                con_b * by_x + con_c * by_y,
                -0.5 * by_xx,
                -by_xy,
                -0.5 * by_yy,
                flat,
            ]
            + [color_sums]
            + [jnp.zeros((7, list_size), f32)],
            axis=0,
        )

    def some_tiles(step, carry):
        slots = range(pair)
        at = [step * pair + slot for slot in slots]
        arrived = [load_tile(tile_at) for tile_at in at]
        passed, gaps, tinted, color_sums, behind = [], [], [], [], []
        for slot in slots:
            alphas_of(slot, *arrived[slot])
            passed.append(jnp.dot(keeps[slot], before[...], preferred_element_type=f32))
            colors_of(slot, at[slot], arrived[slot][0])
        for slot in slots:
            weights_of(slot, passed[slot])
            gaps.append(
                lax.dot_general(
                    painted[slot], paints[slot], (((1,), (1,)), ((), ())), preferred_element_type=f32
                )
            )
        for slot in slots:
            signs = signs_of(gaps[slot] + pltpu.roll(gaps[slot], 64, 1))
            tinted.append(jnp.dot(signs.astype(bf16), tints[slot], preferred_element_type=f32))
            color_sums.append(color_grads(slot, signs))
        for slot in slots:
            flows_of(slot, tinted[slot])
            behind.append(jnp.dot(suffix[slot], after[...], preferred_element_type=f32))
        owners, pieces = [], []
        for slot in slots:
            grads = grads_of(slot, *arrived[slot], behind[slot], color_sums[slot])
            high = grads.astype(bf16).astype(f32)
            pieces.append(jnp.concatenate([high, grads - high], axis=0))
            ids = lists_ref[pl.ds(at[slot], 1), :]
            owners.append(wide(ids >> 8))
            lanes = slice(slot * list_size, (slot + 1) * list_size)
            one_hot[:, lanes] = (column_ids == (ids & 255)).astype(f32).astype(bf16)

        def spread_group(group_at, carry):
            for slot in slots:
                lanes = slice(slot * list_size, (slot + 1) * list_size)
                for block in range(group):
                    mask = owners[slot] == group_at * group + block
                    mask = jnp.concatenate([mask, mask], axis=0)
                    chosen[block * 32 : block * 32 + 32, lanes] = jnp.where(
                        mask, pieces[slot], 0.0
                    ).astype(bf16)
            spread[group_at] += lax.dot_general(
                chosen[...], one_hot[...], (((1,), (1,)), ((), ())), preferred_element_type=f32
            )
            return carry

        if spread.shape[0] == 1:
            spread_group(0, 0)
        else:
            lax.fori_loop(0, spread.shape[0], spread_group, 0)
        return carry

    lax.fori_loop(0, tile_dev // pair, some_tiles, 0)

    def finish_group(group_at, carry):
        for block in range(group):
            both = spread[group_at, block * 32 : block * 32 + 32, :]
            total = both[0:16] + both[16:32]
            for half in range(2):
                chunk = block * 2 + half
                owner = group_at * (2 * group // per_owner) + chunk // per_owner
                lanes = chunk % per_owner * 128
                dense_ref[owner % tile_groups, owner // tile_groups, :, lanes : lanes + 128] = total[
                    0:9, half * 128 : half * 128 + 128
                ]
        return carry

    if spread.shape[0] == 1:
        finish_group(0, 0)
    else:
        lax.fori_loop(0, spread.shape[0], finish_group, 0)

    sent_grads = [
        send(
            dense_ref.at[tiles[step], views[turn]],
            landing_ref.at[turn, step],
            grads_send.at[turn, step],
            grads_recv.at[turn, step],
            (views[turn], tiles[step]),
        )
        for turn, step in steps
    ]
    totals = [None] * view_count
    totals[0] = dense_ref[pl.ds(tiles[0], 1), pl.ds(views[0], 1)][0, 0]
    for copy, (turn, step) in zip(sent_grads, steps):
        copy.wait()
        block = landing_ref[turn, step]
        totals[turn] = block if totals[turn] is None else totals[turn] + block
    for turn in range(view_count):
        sender = views[(view_count - turn) % view_count]
        out_ref[pl.ds(sender, 1)] = totals[turn][None]


def update_kernel(
    width,
    height,
    cameras_ref,
    rates_ref,
    grads_ref,
    params_ref,
    first_ref,
    second_ref,
    new_params_ref,
    new_first_ref,
    new_second_ref,
):
    camera = camera_columns(cameras_ref)
    values = [params_ref[at : at + 1, :] for at in range(59)]
    _, pullback = jax.vjp(
        lambda rows: project(rows, camera, float(width), 0.5 * width, 0.5 * height), values
    )
    given = [grads_ref[:, row_at, :] for row_at in range(9)]
    grads = list(pullback(tuple(given[:5] + given[6:]))[0])
    grads[10] = jnp.sum(given[5], axis=0, keepdims=True) * (1.0 - sigmoid(values[10]))
    for at in range(59):
        new_first_ref[at : at + 1, :] = grads[at]
    gradient = new_first_ref[...]
    new_first = beta_one * first_ref[...] + (1.0 - beta_one) * gradient
    new_second = beta_two * second_ref[...] + (1.0 - beta_two) * gradient * gradient
    new_first_ref[...] = new_first
    new_second_ref[...] = new_second
    step_size = rates_ref[...] * (new_first / (1.0 - beta_one**ADAM_STEP))
    new_params_ref[...] = params_ref[...] - step_size / (
        jnp.sqrt(new_second / (1.0 - beta_two**ADAM_STEP)) + adam_eps
    )


def in_vmem(count):
    return [pl.BlockSpec(memory_space=pltpu.VMEM)] * count


def per_device(params, first_moment, second_moment, cameras, target, lists, lengths):
    f32, bf16 = jnp.float32, jnp.bfloat16
    view_count = lax.axis_size("views")
    tile_groups = lax.axis_size("tiles")
    peers = view_count * tile_groups
    owned = params.shape[1]
    tile_dev = target.shape[1]
    list_size = lists.shape[2]
    pixels = target.shape[3]
    width = TILE_COLS * TILE_SIDE
    height = tile_dev * tile_groups // TILE_COLS * TILE_SIDE
    limit = 56 * 1024 * 1024

    dma = pltpu.SemaphoreType.DMA
    semaphores = [dma((view_count, tile_groups))] * 4
    by_owner = (tile_groups, view_count, 9, owned)
    block_rows = (view_count, 9, owned)
    blocks = peers * owned // 256
    group = 16
    pair = 8
    row_grads = pl.pallas_call(
        lambda *refs: step_kernel(width, height, *refs),
        out_shape=jax.ShapeDtypeStruct(block_rows, f32),
        in_specs=[pl.BlockSpec(memory_space=pltpu.SMEM)]
        + [pl.BlockSpec(memory_space=pltpu.HBM)] * 4,
        out_specs=pl.BlockSpec(memory_space=pltpu.VMEM),
        scratch_shapes=[
            pltpu.VMEM(cameras.shape, f32),
            pltpu.VMEM(params.shape, f32),
            pltpu.VMEM(lists.shape[1:], jnp.int32),
            pltpu.VMEM((3, tile_dev, pixels), f32),
            dma((4,)),
            pltpu.VMEM(block_rows, f32),
            pltpu.VMEM(by_owner, f32),
            pltpu.VMEM(by_owner, f32),
            pltpu.VMEM((view_count, tile_groups, 9, owned), f32),
        ]
        + semaphores
        + [
            pltpu.VMEM((9, tile_dev, list_size), f32),
            pltpu.VMEM((pair, pixels, 2 * list_size), bf16),
            pltpu.VMEM((pair, pixels, list_size), bf16),
            pltpu.VMEM((2 * list_size, list_size), bf16),
            pltpu.VMEM((list_size, list_size), bf16),
            pltpu.VMEM((pair, pixels, list_size), f32),
            pltpu.VMEM((pair, pixels, list_size), f32),
            pltpu.VMEM((pair, pixels, list_size), f32),
            pltpu.VMEM((pair, pixels, list_size), f32),
            pltpu.VMEM((pair, pixels, 2 * list_size + 128), bf16),
            pltpu.VMEM((pair, 128, 2 * list_size + 128), bf16),
            pltpu.VMEM((pair, 128, list_size), bf16),
            pltpu.VMEM((group * 32, pair * list_size), bf16),
            pltpu.VMEM((256, pair * list_size), bf16),
            pltpu.VMEM((blocks // group, group * 32, 256), f32),
        ],
        compiler_params=pltpu.CompilerParams(
            collective_id=0, has_side_effects=True, vmem_limit_bytes=limit
        ),
        name="splat_gradients",
    )(lengths[0], cameras, params, lists[0], target[0].transpose(1, 0, 2))

    like = jax.ShapeDtypeStruct(params.shape, f32)
    return pl.pallas_call(
        lambda *refs: update_kernel(width, height, *refs),
        out_shape=(like, like, like),
        in_specs=in_vmem(6),
        out_specs=tuple(in_vmem(3)),
        compiler_params=pltpu.CompilerParams(vmem_limit_bytes=limit),
        name="update_gaussians",
    )(cameras, jnp.asarray(learning), row_grads, params, first_moment, second_moment)


def solution(mesh):
    placed = (
        P(None, ("views", "tiles")),
        P(None, ("views", "tiles")),
        P(None, ("views", "tiles")),
        P(),
        P("views", "tiles", None, None),
        P("views", "tiles", None),
        P("views", "tiles"),
    )
    return jax.shard_map(
        per_device,
        mesh=mesh,
        in_specs=placed,
        out_specs=(
            P(None, ("views", "tiles")),
            P(None, ("views", "tiles")),
            P(None, ("views", "tiles")),
        ),
        check_vma=False,
    )
```
